512 devices in a mesh: dp: 8 (over y), ta: 16 (over z_lo, x), ha: 4 (over z_hi, core).
Axes of the slice: x: 4, y: 8, z: 8 (z_hi: 2, z_lo: 4; z = z_hi * 4 + z_lo), core: 2. Of those that a mesh axis runs over, the one named last changes fastest.
Arguments:
- decoder_feature_rows: bfloat16 [32768, 768], P(('dp', 'ta', 'ha')), parts along dimension 0, may hold values from -12 to 12
- slot_row_index: int32 [32768], P('dp'), parts along dimension 0, may hold values from 0 to 4095, as said below
- latent_frame_count: int32 [48], P('dp'), parts along dimension 0, may hold values from 1 to 81, 256 in all
- first_norm_gain: float32 [384], replicated, may hold values from 0.1 to 1.9
- first_norm_bias: float32 [384], replicated, may hold values from -3 to 3
- first_convolution_weight: bfloat16 [3, 3, 3, 384, 384], P(None, None, None, 'ha'), may hold values from -0.0625 to 0.0625
- first_convolution_bias: float32 [384], replicated, may hold values from -3 to 3
- second_norm_gain: float32 [384], replicated, may hold values from 0.1 to 1.9
- second_norm_bias: float32 [384], replicated, may hold values from -3 to 3
- second_convolution_weight: bfloat16 [3, 3, 3, 384, 384], P(None, None, None, 'ha'), may hold values from -0.0625 to 0.0625
- second_convolution_bias: float32 [384], replicated, may hold values from -3 to 3
Outputs:
- decoded: bfloat16 [2048, 16, 2, 384], P(('dp', 'ta'), 'ha'), parts along dimension 0
The draws below stay inside these ranges and needn't reach their ends.
There are 8 independent parts, one for each index of `dp`. The reference program is written for one: setup_inputs(seed, part) draws one part's arguments, and reference() takes and returns one part's arrays. A program takes and returns all parts, laid end to end along the dimension named above; an argument that names none is the same for every part. Nothing has to cross between parts.
Inputs may be any that keep to these rules, and one draw needn't show every extreme that they name: `slot_row_index`: A permutation of 0 to 4095. Slot i lies on the device of flat index i // 64 over ta+ha; row g is owned by the device of ta index (g // 16) // 16 and ha index (g % 16) // 4. The slots of one device hold at most 2 rows of any one owner, and exactly 2 of some owner.
All inputs are finite; a program needn't handle non-finite values.
Results may differ from the reference program's by a relative error of at most 0.0042.
Values may be sent and summed in bfloat16 or wider, within the bound.
No kernel may reach another device: no remote copies, remote signals or barrier semaphores. Data moves between devices by JAX's collectives and lax.ppermute only.
A program may use at most 64 MiB of HBM per device.

```python
import math
import jax
import jax.numpy as jnp
import numpy as np
from jax import lax

CH = 384
GROUPS = 32
F_DEV = 16
R_DEV = 4
COLS = 2
NF = 256
NROWS = 4096
VIDEOS = 6
MOST_FRAMES = 81
N_TA = 16
N_HA = 4


def make_plan(key):
    devices = N_TA * N_HA
    number_of_slots = F_DEV * R_DEV
    total = devices * number_of_slots
    key_order, key_bump, key_shuffle, key_score = jax.random.split(key, 4)
    order_seq = jax.random.permutation(key_order, number_of_slots).astype(jnp.int32)
    offsets = order_seq % devices
    bump = jax.random.randint(key_bump, (), 0, devices - 1).astype(jnp.int32)
    offsets = offsets.at[0].set((offsets[0] + 1 + bump) % devices)
    source = jnp.arange(devices, dtype=jnp.int32)[:, None]
    shuffle_keys = jax.random.split(key_shuffle, devices)
    shuffles = jax.vmap(lambda sub_key: jax.random.permutation(sub_key, number_of_slots))(shuffle_keys).astype(jnp.int32)
    owners = ((source + offsets[shuffles]) % devices).reshape(-1)
    score = jax.random.permutation(key_score, total).astype(jnp.int32)
    sorted_ids = jnp.argsort(owners * total + score, stable=True).astype(jnp.int32)
    ranking = jnp.zeros((total,), jnp.int32).at[sorted_ids].set(jnp.arange(total, dtype=jnp.int32))
    places = ranking - owners * number_of_slots
    frame_of = owners // N_HA * F_DEV + places // R_DEV
    row_in = owners % N_HA * R_DEV + places % R_DEV
    return (frame_of * (R_DEV * N_HA) + row_in).astype(jnp.int32)


def draw_slot_row_index(key, part):
    return make_plan(key)


def draw_decoder_feature_rows(key, part):
    row_ids = make_plan(key)
    key = jax.random.fold_in(key, 7)
    key_base, key_chan = jax.random.split(key, 2)
    image_height = R_DEV * N_HA
    row_scale = 0.5 + (row_ids % image_height).astype(jnp.float32) / (image_height - 1)
    base = jnp.clip(jax.random.normal(key_base, (NROWS, COLS, CH), jnp.float32), -4.0, 4.0)
    chan_scale = jnp.exp(jax.random.uniform(key_chan, (CH,), jnp.float32, math.log(0.2), math.log(2.0)))
    values = base * chan_scale * row_scale[:, None, None]
    return values.reshape(NROWS, COLS * CH).astype(jnp.bfloat16)


def levels(own_key, shape, shards, smallest, top_value):
    loudness, own = 1.0, jax.random.fold_in(own_key, 6)
    for axis_at, shards_of in shards:
        draws = jnp.exp(jax.random.uniform(jax.random.fold_in(own, axis_at), (shards_of,), jnp.float32, smallest / len(shards), top_value / len(shards)))
        loudness = loudness * jnp.repeat(draws, shape[axis_at] // shards_of).reshape([-1 if axis == axis_at else 1 for axis in range(len(shape))])
    return loudness


def profile(count, total, limit, slope):
    loads = [(1 << 20) // math.isqrt(rank ** slope) + 1 for rank in range(2, count + 1)]
    rest, given = total - limit - (count - 1), [1] * (count - 1)
    while rest > 0:
        free = [i for i in range(count - 1) if given[i] < limit]
        pool, budget = sum([loads[i] for i in free]), rest
        for i in free:
            extra = min(limit - given[i], max(1, budget * loads[i] // pool), rest)
            given[i] = given[i] + extra
            rest = rest - extra
    return np.array([limit] + given)


def uneven(stream_key, count, total, bound, slope):
    if count == 2:
        one = jax.random.randint(stream_key, (), max(1, total - bound), min(bound, total - 1) + 1)
        return jnp.stack([one, total - one])
    sizes = jnp.asarray(profile(count, total, bound, slope), jnp.int32)
    couples = (count - 1) // 2
    giver, receiver = sizes[1:1 + 2 * couples:2], sizes[2:2 + 2 * couples:2]
    room = jnp.minimum(giver - 1, bound - receiver)
    passed = jax.random.randint(jax.random.fold_in(stream_key, 1), (couples,), 0, 1 << 20) % (room + 1)
    sizes = sizes.at[1:1 + 2 * couples:2].set(giver - passed).at[2:2 + 2 * couples:2].set(receiver + passed)
    return sizes[jax.random.permutation(jax.random.fold_in(stream_key, 2), count)]


def gaussian(key, shape, deviation, reach, cuts=(), kind=jnp.bfloat16):
    values = jax.random.normal(key, shape, jnp.float32) * deviation
    if len(cuts) > 0:
        values = levels(key, shape, cuts, -0.22, 0.18) * values
    return jnp.clip(values, min=-reach, max=reach).astype(kind)


def setup_inputs(seed: int = 0, part: int = 0) -> dict:
    splits = jax.random.split(jax.random.key(seed), 12)
    part_splits = jax.random.split(jax.random.fold_in(splits[11], part), 12)
    return {
        "decoder_feature_rows": draw_decoder_feature_rows(jax.random.fold_in(jax.random.fold_in(splits[11], part), 71), part),
        "slot_row_index": draw_slot_row_index(jax.random.fold_in(jax.random.fold_in(splits[11], part), 71), part),
        "latent_frame_count": uneven(part_splits[2], VIDEOS, NF, MOST_FRAMES, 2).astype(jnp.int32),
        "first_norm_gain": jnp.clip(1.0 + 0.18 * jax.random.normal(splits[3], (CH,), jnp.float32), 0.1, 1.9),
        "first_norm_bias": gaussian(splits[4], (CH,), 0.5, 3.0, (), jnp.float32),
        "first_convolution_weight": gaussian(splits[5], (3, 3, 3, CH, CH), (27 * CH) ** -0.5, 0.0625, ((3, 4),)),
        "first_convolution_bias": gaussian(splits[6], (CH,), 0.5, 3.0, (), jnp.float32),
        "second_norm_gain": jnp.clip(1.0 + 0.18 * jax.random.normal(splits[7], (CH,), jnp.float32), 0.1, 1.9),
        "second_norm_bias": gaussian(splits[8], (CH,), 0.5, 3.0, (), jnp.float32),
        "second_convolution_weight": gaussian(splits[9], (3, 3, 3, CH, CH), (27 * CH) ** -0.5, 0.0625, ((3, 4),)),
        "second_convolution_bias": gaussian(splits[10], (CH,), 0.5, 3.0, (), jnp.float32),
    }


def group_sums(values, groups):
    extent = values.shape
    grouped = values.reshape(extent[0], extent[1] * extent[2], groups, extent[3] // groups)
    return (lax.optimization_barrier(jnp.sum(grouped, axis=(1, 3))), lax.optimization_barrier(jnp.sum(grouped * grouped, axis=(1, 3))))

def normalize(values, totals, squares, entries, gain_vec, offset, groups):
    average = totals / entries
    spread = squares / entries - average * average
    inverse = lax.rsqrt(spread + 1e-06)
    extent = values.shape
    grouped = values.reshape(extent[0], extent[1], extent[2], groups, extent[3] // groups)
    centred = (grouped - average[:, None, None, :, None]) * inverse[:, None, None, :, None]
    scaled = centred.reshape(extent) * gain_vec + offset
    return jax.nn.silu(scaled).astype(jnp.bfloat16)

def causal_conv(act, weight, masks):
    frames, image_height, columns, channels = act.shape
    outputs = weight.shape[3]
    padded = jnp.pad(act.astype(jnp.float32), ((2, 0), (1, 1), (1, 1), (0, 0)))
    total = jnp.zeros((frames * image_height * columns, outputs), jnp.float32)
    for time_tap in range(3):
        window = padded[time_tap:time_tap + frames] * masks[time_tap][:, None, None, None]
        for row_tap in range(3):
            for col_tap in range(3):
                piece = window[:, row_tap:row_tap + image_height, col_tap:col_tap + columns].reshape(-1, channels)
                kernel = weight[time_tap, row_tap, col_tap].astype(jnp.float32).T
                total = total + jnp.dot(piece, kernel, precision=lax.Precision.HIGHEST)
    return total.reshape(frames, image_height, columns, outputs)

def reference(decoder_feature_rows, slot_row_index, latent_frame_count, first_norm_gain, first_norm_bias, first_convolution_weight, first_convolution_bias, second_norm_gain, second_norm_bias, second_convolution_weight, second_convolution_bias):
    image_height = R_DEV * N_HA
    frames = F_DEV * N_TA
    dispersed_rows = jnp.zeros_like(decoder_feature_rows).at[slot_row_index].set(decoder_feature_rows)
    latent = dispersed_rows.reshape(frames, image_height, COLS, CH)
    frame_ids = jnp.arange(frames, dtype=jnp.int32)
    video_ends = jnp.cumsum(latent_frame_count).astype(jnp.int32)
    starts = lax.optimization_barrier(jnp.sum(jnp.where(video_ends[None, :] <= frame_ids[:, None], latent_frame_count[None, :], 0), axis=1)).astype(jnp.int32)
    masks = jnp.stack([(frame_ids - 2 + time_tap >= starts).astype(jnp.float32) for time_tap in range(3)])
    entries = image_height * COLS * (CH // GROUPS)
    latent_float = latent.astype(jnp.float32)
    totals, squares = group_sums(latent_float, GROUPS)
    first_act = normalize(latent_float, totals, squares, entries, first_norm_gain, first_norm_bias, GROUPS)
    hidden = (causal_conv(first_act, first_convolution_weight, masks) + first_convolution_bias).astype(jnp.bfloat16)
    hidden_float = hidden.astype(jnp.float32)
    totals, squares = group_sums(hidden_float, GROUPS)
    second_act = normalize(hidden_float, totals, squares, entries, second_norm_gain, second_norm_bias, GROUPS)
    return (causal_conv(second_act, second_convolution_weight, masks) + second_convolution_bias + latent_float).astype(jnp.bfloat16)
```

```python
import functools

import jax
import jax.numpy as jnp
from jax import lax
from jax.experimental import pallas as pl
from jax.experimental.pallas import tpu as pltpu
from jax.sharding import PartitionSpec as P

CH = 384
WIDE = 768
GROUP = 12
ROWS = 16
OWN = 96
PAIR = 192
F_DEV = 16
BLOCK = 256
SLOTS = 64
CAP = 8
VIDEOS = 6
F32, BF16, I32 = jnp.float32, jnp.bfloat16, jnp.int32
VMEM_LIMIT = 24 * 2**20


def dot(a, b):
    return jnp.dot(a, b, preferred_element_type=F32)


def dot_nt(a, b):
    return lax.dot_general(a, b, (((1,), (1,)), ((), ())), preferred_element_type=F32)


def iota(shape, axis):
    return lax.broadcasted_iota(I32, shape, axis)


def twelfth(v):
    return (v * 43691) >> 19


def three(v):
    high = v.astype(BF16)
    rest = v - high.astype(F32)
    middle = rest.astype(BF16)
    low = (rest - middle.astype(F32)).astype(BF16)
    return high, middle, low


def pack_kernel(at_ref, plan_ref, rows_ref, out_ref):
    own = at_ref[0] * 4 + at_ref[1]
    ids = plan_ref[pl.ds(own // 2, 1), :]
    ids = jnp.where(own % 2 == 1, pltpu.roll(ids, 64, 1), ids)
    block = ids >> 8
    hit = iota((16, 128), 0) == block
    before = dot(hit.astype(BF16), (iota((128, 128), 0) < iota((128, 128), 1)).astype(BF16))
    rank = jnp.sum(jnp.where(hit, before, 0.0), axis=0, keepdims=True)
    position = block * CAP + rank.astype(I32)
    place = iota((256, 128), 0)
    hot = ((place >> 4) * CAP + (place & 7) == position).astype(BF16)
    out_ref[...] = dot(hot[:, :SLOTS], rows_ref[...]).astype(BF16)


def table_kernel(at_ref, plan_ref, out_ref):
    plan = plan_ref[...]
    match = (plan >> 8) == at_ref[0]
    i, j = iota((128, 128), 0), iota((128, 128), 1)
    before = dot(match.astype(BF16), ((i < j) & ((i >> 6) == (j >> 6))).astype(BF16))
    value = jnp.where(match, (plan & 255) + 1, 0).astype(F32)
    ranked = jnp.concatenate([jnp.where(before == k, value, 0.0) for k in range(CAP)], axis=0)
    half = ((iota((8, 128), 1) >> 6) == iota((8, 128), 0)).astype(BF16)
    held = dot_nt(half, ranked.astype(BF16))
    q, p = iota((256, 256), 0), iota((256, 256), 1)
    held = dot(held.astype(BF16), (q == (p & 7) * 32 + (p >> 3)).astype(BF16))
    want = (q + 1).astype(F32)
    out_ref[:, 0:256] = (held[0:1] == want).astype(BF16)
    out_ref[:, 256:512] = (held[1:2] == want).astype(BF16)


def unpack_kernel(table_ref, packed_ref, out_ref, tail_ref):
    rows = dot(table_ref[...], packed_ref[...]).astype(BF16)
    out_ref[...] = rows
    tail_ref[...] = rows[BLOCK - 64 :]


def frame_stats(values, width):
    rows = values.shape[0]
    pick = ((iota((16, rows), 1) >> 4) == iota((16, rows), 0)).astype(BF16)
    wide = values.astype(F32)
    square = wide * wide
    high = square.astype(BF16)
    low = (square - high.astype(F32)).astype(BF16)
    sums = dot(pick, values)
    squares = dot(pick, high) + dot(pick, low)
    if width == WIDE:
        sums = sums[:, :CH] + sums[:, CH:]
        squares = squares[:, :CH] + squares[:, CH:]
        lanes = CH
        first, second = iota((CH, CH), 0), iota((CH, CH), 1)
    else:
        lanes = PAIR
        first, second = iota((PAIR, PAIR), 0), iota((PAIR, PAIR), 1)
        first = jnp.where(first >= OWN, first - OWN, first)
        second = jnp.where(second >= OWN, second - OWN, second)
    same = (twelfth(first) == twelfth(second)).astype(BF16)
    both = jnp.concatenate([sums, squares], axis=0)
    total = sum(dot(part, same) for part in three(both))
    entries = ROWS * 2 * GROUP
    mean = total[0:16] / entries
    var = total[16:32] / entries - mean * mean
    return mean, lax.rsqrt(var + 1e-06)


def silu(v):
    return v / (1.0 + jnp.exp(-v))


def store_taps(taps_ref, at, act):
    row = iota((ROWS, WIDE), 0)
    taps_ref[0, at : at + ROWS, :] = jnp.where(row == 0, 0.0, pltpu.roll(act, 1, 0)).astype(BF16)
    taps_ref[1, at : at + ROWS, :] = act.astype(BF16)
    taps_ref[2, at : at + ROWS, :] = jnp.where(row == ROWS - 1, 0.0, pltpu.roll(act, ROWS - 1, 0)).astype(BF16)


def norm_first(rows_ref, gain, bias, taps_ref, at):
    frames = rows_ref.shape[0] // ROWS
    mean, inverse = frame_stats(rows_ref[...], WIDE)
    for f in range(frames):
        value = rows_ref[f * ROWS : (f + 1) * ROWS, :].astype(F32)
        m, s = mean[f : f + 1], inverse[f : f + 1]
        halves = [
            silu((value[:, c * CH : (c + 1) * CH] - m) * s * gain + bias) for c in range(2)
        ]
        store_taps(taps_ref, at + f * ROWS, jnp.concatenate(halves, axis=1))


def convolve(taps_ref, weight_ref, rows, first_frame, count_ref):
    totals = []
    for a in range(3):
        acc = None
        for b in range(3):
            for c in range(2):
                part = dot_nt(
                    taps_ref[b, a * ROWS : a * ROWS + rows, c * CH : (c + 1) * CH],
                    weight_ref[3 * a + b, c * OWN : c * OWN + PAIR, :],
                )
                acc = part if acc is None else acc + part
        totals.append(acc)
    frame = first_frame + (iota((rows, 1), 0) >> 4)
    start = jnp.zeros((rows, 1), I32)
    end = jnp.int32(0)
    for v in range(VIDEOS):
        count = count_ref[v]
        end = end + count
        start = start + jnp.where(frame >= end, count, 0)
    total = totals[2]
    for a in range(2):
        total = total + totals[a] * jnp.where(frame - 2 + a >= start, 1.0, 0.0)
    return total


def norm_second(hidden, gain, bias, out_ref, at):
    mean, inverse = frame_stats(hidden, PAIR)
    for f in range(hidden.shape[0] // ROWS):
        value = hidden[f * ROWS : (f + 1) * ROWS].astype(F32)
        act = silu((value - mean[f : f + 1]) * inverse[f : f + 1] * gain + bias)
        out_ref[at + f * ROWS : at + (f + 1) * ROWS, :] = act.astype(BF16)


def main_kernel(at_ref, count_ref, rows_ref, wide_ref, own_ref, weight_ref, act_ref, rest_ref, taps_ref):
    base = at_ref[0] * F_DEV
    norm_first(rows_ref, wide_ref[0:1], wide_ref[1:2], taps_ref, 0)
    rows = BLOCK - 2 * ROWS
    hidden = convolve(taps_ref, weight_ref, rows, base + 2, count_ref) + own_ref[0:1]
    norm_second(hidden.astype(BF16), own_ref[1:2], own_ref[2:3], act_ref, 0)
    lane = iota((WIDE, PAIR), 1)
    source = at_ref[1] * OWN + jnp.where(lane < OWN, CH + lane, lane - OWN)
    own = (iota((WIDE, PAIR), 0) == source).astype(BF16)
    rest_ref[...] = dot(rows_ref[...], own).astype(BF16)


def halo_kernel(at_ref, count_ref, earlier_ref, rows_ref, wide_ref, own_ref, weight_ref, main_ref, act_ref, taps_ref, join_ref):
    base = at_ref[0] * F_DEV
    join_ref[0:64, :] = earlier_ref[...]
    join_ref[64:96, :] = rows_ref[0:32, :]
    norm_first(join_ref, wide_ref[0:1], wide_ref[1:2], taps_ref, 0)
    hidden = convolve(taps_ref, weight_ref, 64, base - 2, count_ref) + own_ref[0:1]
    norm_second(hidden.astype(BF16), own_ref[1:2], own_ref[2:3], act_ref, 0)
    act_ref[64:288, :] = main_ref[...]


def last_kernel(at_ref, count_ref, act_ref, rest_ref, own_ref, weight_ref, out_ref, taps_ref):
    for f in range(F_DEV + 2):
        parts = [act_ref[h, f * ROWS : (f + 1) * ROWS, :].astype(F32) for h in range(4)]
        whole = jnp.concatenate([p[:, OWN:] for p in parts] + [p[:, :OWN] for p in parts], axis=1)
        store_taps(taps_ref, f * ROWS, whole)
    total = convolve(taps_ref, weight_ref, BLOCK, at_ref[0] * F_DEV, count_ref)
    total = (total + own_ref[3:4] + rest_ref[...].astype(F32)).astype(BF16)
    to, at = iota((BLOCK, BLOCK), 0), iota((BLOCK, BLOCK), 1)
    order = (((to >> 2) & 15) * ROWS + (to >> 6) * 4 + (to & 3) == at).astype(BF16)
    out_ref[...] = dot(order, total).astype(BF16)


def join_kernel(parts_ref, out_ref):
    parts = [parts_ref[h].astype(F32) for h in range(4)]
    zero = jnp.concatenate([p[:, OWN:] for p in parts], axis=1)
    one = jnp.concatenate([p[:, :OWN] for p in parts], axis=1)
    out_ref[...] = jnp.stack([zero, one], axis=1).astype(BF16).reshape(F_DEV, 4, 2, CH)


def call(kernel, shapes, n_scalars, n_arrays, scratch=(), flops=0, **more):
    many = isinstance(shapes, (list, tuple))
    out_shape = [jax.ShapeDtypeStruct(s, BF16) for s in shapes] if many else shapes
    return pl.pallas_call(
        kernel,
        out_shape=out_shape,
        in_specs=[pl.BlockSpec(memory_space=pltpu.SMEM)] * n_scalars
        + [pl.BlockSpec(memory_space=pltpu.VMEM)] * n_arrays,
        out_specs=[pl.BlockSpec(memory_space=pltpu.VMEM)] * len(out_shape),
        scratch_shapes=[pltpu.VMEM(s, BF16) for s in scratch],
        compiler_params=pltpu.CompilerParams(vmem_limit_bytes=VMEM_LIMIT),
        cost_estimate=pl.CostEstimate(flops=flops, bytes_accessed=2**20, transcendentals=0),
        **more,
    )


def local(
    decoder_feature_rows,
    slot_row_index,
    latent_frame_count,
    first_norm_gain,
    first_norm_bias,
    first_convolution_weight,
    first_convolution_bias,
    second_norm_gain,
    second_norm_bias,
    second_convolution_weight,
    second_convolution_bias,
):
    ta, ha = lax.axis_index("ta"), lax.axis_index("ha")
    at = jnp.stack([ta, ha]).astype(I32)
    plan = slot_row_index.reshape(32, 128)
    n_ta = lax.axis_size("ta")
    same_core = [[t * 4 + z * 2 + c for t in range(n_ta) for z in range(2)] for c in range(2)]
    chips = [[0, 1], [2, 3]]

    [packed] = call(pack_kernel, [(256, WIDE)], 1, 2, flops=10**7)(at, plan, decoder_feature_rows)
    arrived = lax.all_to_all(
        packed.reshape(32, CAP, WIDE), ("ta", "ha"), 0, 0, axis_index_groups=same_core, tiled=True
    ).reshape(256, WIDE)
    [table] = call(table_kernel, [(BLOCK, 512)], 1, 1, flops=10**7)(at, plan)
    wide = jnp.stack([first_norm_gain, first_norm_bias])
    own = jnp.stack([first_convolution_bias, second_norm_gain, second_norm_bias, second_convolution_bias])
    own = lax.dynamic_slice_in_dim(own, ha * OWN, OWN, 1)
    own = jnp.concatenate([own, own], axis=1)
    first = first_convolution_weight.reshape(9, 3 * OWN, CH)
    second = second_convolution_weight.reshape(9, 3 * OWN, CH)
    both = lax.all_gather(arrived, "ha", axis=0, axis_index_groups=chips, tiled=True)
    rows, tail = call(unpack_kernel, [(BLOCK, WIDE), (64, WIDE)], 0, 2, flops=10**8)(table, both)
    earlier = lax.ppermute(tail, "ta", [(i, i + 1) for i in range(n_ta - 1)])
    act, rest = call(
        main_kernel, [(224, PAIR), (BLOCK, PAIR)], 2, 4, [(3, BLOCK, WIDE)], flops=2 * 10**9
    )(at, latent_frame_count, rows, wide, own, first)
    [act] = call(
        halo_kernel, [(288, PAIR)], 2, 6, [(3, 96, WIDE), (96, WIDE)], flops=10**9
    )(at, latent_frame_count, earlier, rows, wide, own, first, act)
    acts = lax.all_gather(act, "ha", axis=0, tiled=False)
    [out] = call(last_kernel, [(BLOCK, PAIR)], 2, 4, [(3, 288, WIDE)], flops=2 * 10**9)(
        at, latent_frame_count, acts, rest, own, second
    )
    parts = lax.all_to_all(out.reshape(4, 64, PAIR), "ha", 0, 0, tiled=True)
    [joined] = call(join_kernel, [(F_DEV, 4, 2, CH)], 0, 1)(parts)
    return joined


def solution(mesh):
    in_specs = (
        P(("dp", "ta", "ha"), None),
        P("dp"),
        P("dp"),
        P(),
        P(),
        P(None, None, None, "ha", None),
        P(),
        P(),
        P(),
        P(None, None, None, "ha", None),
        P(),
    )
    out_specs = P(("dp", "ta"), "ha", None, None)
    return jax.shard_map(local, mesh=mesh, in_specs=in_specs, out_specs=out_specs, check_vma=False)
```

```python
import jax
import jax.numpy as jnp
from jax import lax
from jax.experimental import pallas as pl
from jax.experimental.pallas import tpu as pltpu
from jax.sharding import PartitionSpec as P

CH = 384
WIDE = 768
GROUP = 12
ROWS = 16
OWN = 96
PAIR = 192
F_DEV = 16
BLOCK = 256
SLOTS = 64
CAP = 8
VIDEOS = 6
F32, BF16, I32 = jnp.float32, jnp.bfloat16, jnp.int32
VMEM_LIMIT = 24 * 2**20


def dot(a, b):
    return jnp.dot(a, b, preferred_element_type=F32)


def dot_nt(a, b):
    return lax.dot_general(a, b, (((1,), (1,)), ((), ())), preferred_element_type=F32)


def iota(shape, axis):
    return lax.broadcasted_iota(I32, shape, axis)


def twelfth(v):
    return (v * 43691) >> 19


def three(v):
    high = v.astype(BF16)
    rest = v - high.astype(F32)
    middle = rest.astype(BF16)
    low = (rest - middle.astype(F32)).astype(BF16)
    return high, middle, low


def place():
    return lax.axis_index("ta"), lax.axis_index("ha")


def pack_kernel(plan_hbm, rows_hbm, out_ref, plan_ref, rows_ref, plan_sem, rows_sem):
    plan_copy = pltpu.make_async_copy(plan_hbm, plan_ref, plan_sem)
    rows_copy = pltpu.make_async_copy(rows_hbm, rows_ref, rows_sem)
    plan_copy.start()
    rows_copy.start()
    ta, ha = place()
    own = ta * 4 + ha
    lower = (iota((128, 128), 0) < iota((128, 128), 1)).astype(BF16)
    spot = iota((256, 128), 0)
    spot = (spot >> 4) * CAP + (spot & 7)
    plan_copy.wait()
    ids = plan_ref[pl.ds(own // 2, 1), :]
    ids = jnp.where(own % 2 == 1, pltpu.roll(ids, 64, 1), ids)
    block = ids >> 8
    hit = iota((16, 128), 0) == block
    before = dot(hit.astype(BF16), lower)
    rank = jnp.sum(jnp.where(hit, before, 0.0), axis=0, keepdims=True)
    hot = (spot == block * CAP + rank.astype(I32)).astype(BF16)
    rows_copy.wait()
    out_ref[...] = dot(hot[:, :SLOTS], rows_ref[...]).astype(BF16)


def same_group(lanes, wrap):
    first, second = iota((lanes, lanes), 0), iota((lanes, lanes), 1)
    if wrap < lanes:
        first = jnp.where(first >= wrap, first - wrap, first)
        second = jnp.where(second >= wrap, second - wrap, second)
    return (twelfth(first) == twelfth(second)).astype(BF16)


def side_by_side(weight_ref, out_ref):
    for tap in range(9):
        for c in range(2):
            part = weight_ref[tap, c * OWN : c * OWN + PAIR, :].astype(F32)
            at = tap * WIDE + c * CH
            out_ref[at : at + CH, :] = part.T.astype(BF16)


def prepare_kernel(
    plan_ref, gain_ref, bias_ref, b1_ref, g2_ref, n2_ref, b2_ref, w1_ref, w2_ref,
    table_ref, wide_ref, own_ref, same_wide_ref, same_own_ref, select_ref, first_ref, second_ref,
):
    ta, ha = place()
    wide_ref[0:1] = gain_ref[...].reshape(1, CH)
    wide_ref[1:2] = bias_ref[...].reshape(1, CH)
    for k, ref in enumerate((b1_ref, g2_ref, n2_ref, b2_ref)):
        value = ref[...].reshape(1, CH)
        part = jnp.zeros((1, OWN), F32)
        for h in range(4):
            part = jnp.where(ha == h, value[:, h * OWN : (h + 1) * OWN], part)
        own_ref[k : k + 1] = jnp.concatenate([part, part], axis=1)
    same_wide_ref[...] = same_group(CH, CH)
    same_own_ref[...] = same_group(PAIR, OWN)
    lane = iota((WIDE, PAIR), 1)
    source = ha * OWN + jnp.where(lane < OWN, CH + lane, lane - OWN)
    select_ref[...] = (iota((WIDE, PAIR), 0) == source).astype(BF16)
    side_by_side(w1_ref, first_ref)
    side_by_side(w2_ref, second_ref)
    plan = plan_ref[...]
    match = (plan >> 8) == ta
    i, j = iota((128, 128), 0), iota((128, 128), 1)
    before = dot(match.astype(BF16), ((i < j) & ((i >> 6) == (j >> 6))).astype(BF16))
    value = jnp.where(match, (plan & 255) + 1, 0).astype(F32)
    ranked = jnp.concatenate([jnp.where(before == k, value, 0.0) for k in range(CAP)], axis=0)
    half = ((iota((8, 128), 1) >> 6) == iota((8, 128), 0)).astype(BF16)
    held = dot_nt(half, ranked.astype(BF16))
    q, p = iota((256, 256), 0), iota((256, 256), 1)
    held = dot(held.astype(BF16), (q == (p & 7) * 32 + (p >> 3)).astype(BF16))
    want = (q + 1).astype(F32)
    table_ref[:, 0:256] = (held[0:1] == want).astype(BF16)
    table_ref[:, 256:512] = (held[1:2] == want).astype(BF16)


def unpack_kernel(table_ref, packed_ref, out_ref, tail_ref):
    rows = dot(table_ref[...], packed_ref[...]).astype(BF16)
    out_ref[...] = rows
    tail_ref[...] = rows[BLOCK - 64 :]


def frame_stats(values, same):
    rows, lanes = values.shape
    pick = ((iota((16, rows), 1) >> 4) == iota((16, rows), 0)).astype(BF16)
    wide = values.astype(F32)
    square = wide * wide
    high = square.astype(BF16)
    low = (square - high.astype(F32)).astype(BF16)
    both = jnp.concatenate([dot(pick, values), dot(pick, high) + dot(pick, low)], axis=0)
    if lanes == WIDE:
        both = both[:, :CH] + both[:, CH:]
    total = dot(jnp.concatenate(three(both), axis=0), same)
    total = total[0:32] + total[32:64] + total[64:96]
    entries = ROWS * 2 * GROUP
    mean = total[0:16] / entries
    var = total[16:32] / entries - mean * mean
    return mean, lax.rsqrt(var + 1e-06)


def silu(v):
    return v / (1.0 + jnp.exp(-v))


def store_taps(taps_ref, at, act):
    row = iota((ROWS, WIDE), 0)
    taps_ref[0, at : at + ROWS, :] = jnp.where(row == 0, 0.0, pltpu.roll(act, 1, 0)).astype(BF16)
    taps_ref[1, at : at + ROWS, :] = act.astype(BF16)
    taps_ref[2, at : at + ROWS, :] = jnp.where(row == ROWS - 1, 0.0, pltpu.roll(act, ROWS - 1, 0)).astype(BF16)


def norm_first(rows_ref, wide_ref, same, taps_ref):
    gain, bias = wide_ref[0:1], wide_ref[1:2]
    mean, inverse = frame_stats(rows_ref[...], same)
    for f in range(rows_ref.shape[0] // ROWS):
        value = rows_ref[f * ROWS : (f + 1) * ROWS, :].astype(F32)
        m, s = mean[f : f + 1], inverse[f : f + 1]
        halves = [
            silu((value[:, c * CH : (c + 1) * CH] - m) * s * gain + bias) for c in range(2)
        ]
        store_taps(taps_ref, f * ROWS, jnp.concatenate(halves, axis=1))


def convolve(taps_ref, weight_ref, rows, first_frame, count_ref):
    totals = []
    for a in range(3):
        acc = None
        for b in range(3):
            part = dot(
                taps_ref[b, a * ROWS : a * ROWS + rows, :],
                weight_ref[(3 * a + b) * WIDE : (3 * a + b + 1) * WIDE, :],
            )
            acc = part if acc is None else acc + part
        totals.append(acc)
    frame = first_frame + (iota((rows, 1), 0) >> 4)
    start = jnp.zeros((rows, 1), I32)
    end = jnp.int32(0)
    for v in range(VIDEOS):
        count = count_ref[v]
        end = end + count
        start = start + jnp.where(frame >= end, count, 0)
    total = totals[2]
    for a in range(2):
        total = total + totals[a] * jnp.where(frame - 2 + a >= start, 1.0, 0.0)
    return total


def fold(values):
    half = values.shape[0] // 2
    rest = values[:, 128:]
    return jnp.concatenate([values[:, :128], jnp.concatenate([rest[:half], rest[half:]], axis=1)], axis=0)


def norm_second(hidden, own_ref, same):
    gain, bias = own_ref[1:2], own_ref[2:3]
    mean, inverse = frame_stats(hidden, same)
    acts = []
    for f in range(hidden.shape[0] // ROWS):
        value = hidden[f * ROWS : (f + 1) * ROWS].astype(F32)
        acts.append(silu((value - mean[f : f + 1]) * inverse[f : f + 1] * gain + bias))
    return fold(jnp.concatenate(acts, axis=0)).astype(BF16)


EDGE = 64
INNER = BLOCK - 2 * ROWS
FOLDED = (EDGE + INNER) * 3 // 2
CUT = EDGE * 3 // 2


def main_kernel(
    count_ref, rows_ref, wide_ref, own_ref, same_wide_ref, same_own_ref, select_ref, weight_ref,
    act_ref, rest_ref, head_ref, taps_ref,
):
    ta, _ = place()
    norm_first(rows_ref, wide_ref, same_wide_ref[...], taps_ref)
    hidden = convolve(taps_ref, weight_ref, INNER, ta * F_DEV + 2, count_ref) + own_ref[0:1]
    act_ref[...] = norm_second(hidden.astype(BF16), own_ref, same_own_ref[...])
    rest_ref[...] = dot(rows_ref[...], select_ref[...]).astype(BF16)
    for b in range(3):
        head_ref[b] = taps_ref[b, 0:32, :]


def halo_kernel(
    count_ref, earlier_ref, head_ref, wide_ref, own_ref, same_wide_ref, same_own_ref, weight_ref, main_ref,
    act_ref, taps_ref,
):
    ta, _ = place()
    norm_first(earlier_ref, wide_ref, same_wide_ref[...], taps_ref)
    for b in range(3):
        taps_ref[b, EDGE : EDGE + 32, :] = head_ref[b]
    hidden = convolve(taps_ref, weight_ref, EDGE, ta * F_DEV - 2, count_ref) + own_ref[0:1]
    act_ref[0:CUT, :] = norm_second(hidden.astype(BF16), own_ref, same_own_ref[...])
    act_ref[CUT:FOLDED, :] = main_ref[...]


def unfolded(ref, h, base, frames, f):
    half = frames // 2
    low = base + frames * ROWS + (f % half) * ROWS
    lane = 64 * (f // half)
    return jnp.concatenate(
        [
            ref[h, base + f * ROWS : base + (f + 1) * ROWS, :].astype(F32),
            ref[h, low : low + ROWS, :].astype(F32)[:, lane : lane + 64],
        ],
        axis=1,
    )


def last_kernel(count_ref, act_ref, rest_ref, own_ref, weight_ref, out_ref, taps_ref):
    ta, _ = place()
    for f in range(F_DEV + 2):
        parts = [
            unfolded(act_ref, h, 0, 4, f) if f < 4 else unfolded(act_ref, h, CUT, 14, f - 4) for h in range(4)
        ]
        whole = jnp.concatenate([p[:, OWN:] for p in parts] + [p[:, :OWN] for p in parts], axis=1)
        store_taps(taps_ref, f * ROWS, whole)
    total = convolve(taps_ref, weight_ref, BLOCK, ta * F_DEV, count_ref)
    total = (total + own_ref[3:4] + rest_ref[...].astype(F32)).astype(BF16)
    to, at = iota((BLOCK, BLOCK), 0), iota((BLOCK, BLOCK), 1)
    order = (((to >> 2) & 15) * ROWS + (to >> 6) * 4 + (to & 3) == at).astype(BF16)
    ordered = dot(order, total)
    for h in range(4):
        out_ref[h] = fold(ordered[h * 64 : (h + 1) * 64]).astype(BF16)


def join_kernel(parts_ref, out_ref):
    parts = []
    for h in range(4):
        part = parts_ref[h].astype(F32)
        rest = jnp.concatenate([part[64:96, 0:64], part[64:96, 64:128]], axis=0)
        parts.append(jnp.concatenate([part[0:64], rest], axis=1))
    zero = jnp.concatenate([p[:, OWN:] for p in parts], axis=1)
    one = jnp.concatenate([p[:, :OWN] for p in parts], axis=1)
    out_ref[...] = jnp.stack([zero, one], axis=1).astype(BF16).reshape(F_DEV, 4, 2, CH)


def call(kernel, outs, ins, scratch=(), flops=0):
    return pl.pallas_call(
        kernel,
        out_shape=[jax.ShapeDtypeStruct(s, t) for s, t in outs],
        in_specs=[pl.BlockSpec(memory_space=m) for m in ins],
        out_specs=[pl.BlockSpec(memory_space=pltpu.VMEM)] * len(outs),
        scratch_shapes=list(scratch),
        compiler_params=pltpu.CompilerParams(vmem_limit_bytes=VMEM_LIMIT),
        cost_estimate=pl.CostEstimate(flops=flops, bytes_accessed=2**20, transcendentals=0),
    )


def local(
    decoder_feature_rows,
    slot_row_index,
    latent_frame_count,
    first_norm_gain,
    first_norm_bias,
    first_convolution_weight,
    first_convolution_bias,
    second_norm_gain,
    second_norm_bias,
    second_convolution_weight,
    second_convolution_bias,
):
    plan = slot_row_index.reshape(32, 128)
    n_ta = lax.axis_size("ta")
    same_core = [[t * 4 + z * 2 + c for t in range(n_ta) for z in range(2)] for c in range(2)]
    chips = [[0, 1], [2, 3]]
    vmem, smem, hbm = pltpu.VMEM, pltpu.SMEM, pltpu.HBM

    [packed] = call(
        pack_kernel,
        [((256, WIDE), BF16)],
        [hbm] * 2,
        [pltpu.VMEM((32, 128), I32), pltpu.VMEM((SLOTS, WIDE), BF16)] + [pltpu.SemaphoreType.DMA] * 2,
        flops=10**7,
    )(plan, decoder_feature_rows)
    arrived = lax.all_to_all(
        packed.reshape(32, CAP, WIDE), ("ta", "ha"), 0, 0, axis_index_groups=same_core, tiled=True
    ).reshape(256, WIDE)
    weight = (9 * WIDE, PAIR)
    table, wide, own, same_wide, same_own, select, first, second = call(
        prepare_kernel,
        [
            ((BLOCK, 512), BF16),
            ((2, CH), F32),
            ((4, PAIR), F32),
            ((CH, CH), BF16),
            ((PAIR, PAIR), BF16),
            ((WIDE, PAIR), BF16),
            (weight, BF16),
            (weight, BF16),
        ],
        [vmem] * 9,
        flops=2 * 10**9,
    )(
        plan,
        first_norm_gain,
        first_norm_bias,
        first_convolution_bias,
        second_norm_gain,
        second_norm_bias,
        second_convolution_bias,
        first_convolution_weight.reshape(9, 3 * OWN, CH),
        second_convolution_weight.reshape(9, 3 * OWN, CH),
    )
    both = lax.all_gather(arrived, "ha", axis=0, axis_index_groups=chips, tiled=True)
    rows, tail = call(unpack_kernel, [((BLOCK, WIDE), BF16), ((64, WIDE), BF16)], [vmem] * 2, flops=10**8)(table, both)
    earlier = lax.ppermute(tail, "ta", [(i, i + 1) for i in range(n_ta - 1)])
    act, rest, head = call(
        main_kernel,
        [((FOLDED - CUT, 128), BF16), ((BLOCK, PAIR), BF16), ((3, 32, WIDE), BF16)],
        [smem] + [vmem] * 7,
        [pltpu.VMEM((3, BLOCK, WIDE), BF16)],
        flops=2 * 10**9,
    )(latent_frame_count, rows, wide, own, same_wide, same_own, select, first)
    [act] = call(
        halo_kernel, [((FOLDED, 128), BF16)], [smem] + [vmem] * 8, [pltpu.VMEM((3, EDGE + 32, WIDE), BF16)], flops=10**9
    )(latent_frame_count, earlier, head, wide, own, same_wide, same_own, first, act)
    acts = lax.all_gather(act, "ha", axis=0, tiled=False)
    [out] = call(
        last_kernel,
        [((4, 96, 128), BF16)],
        [smem] + [vmem] * 4,
        [pltpu.VMEM((3, EDGE + INNER, WIDE), BF16)],
        flops=2 * 10**9,
    )(latent_frame_count, acts, rest, own, second)
    parts = lax.all_to_all(out, "ha", 0, 0, tiled=True)
    [joined] = call(join_kernel, [((F_DEV, 4, 2, CH), BF16)], [vmem])(parts)
    return joined


def solution(mesh):
    in_specs = (
        P(("dp", "ta", "ha"), None),
        P("dp"),
        P("dp"),
        P(),
        P(),
        P(None, None, None, "ha", None),
        P(),
        P(),
        P(),
        P(None, None, None, "ha", None),
        P(),
    )
    out_specs = P(("dp", "ta"), "ha", None, None)
    return jax.shard_map(local, mesh=mesh, in_specs=in_specs, out_specs=out_specs, check_vma=False)
```

```python
import jax
import jax.numpy as jnp
from jax import lax
from jax.experimental import pallas as pl
from jax.experimental.pallas import tpu as pltpu
from jax.sharding import PartitionSpec as P

CH = 384
WIDE = 768
GROUP = 12
ROWS = 16
OWN = 96
PAIR = 192
F_DEV = 16
BLOCK = 256
SLOTS = 64
CAP = 8
VIDEOS = 6
F32, BF16, I32 = jnp.float32, jnp.bfloat16, jnp.int32
VMEM_LIMIT = 24 * 2**20


def dot(a, b):
    return jnp.dot(a, b, preferred_element_type=F32)


def dot_nt(a, b):
    return lax.dot_general(a, b, (((1,), (1,)), ((), ())), preferred_element_type=F32)


def iota(shape, axis):
    return lax.broadcasted_iota(I32, shape, axis)


def twelfth(v):
    return (v * 43691) >> 19


def three(v):
    high = v.astype(BF16)
    rest = v - high.astype(F32)
    middle = rest.astype(BF16)
    low = (rest - middle.astype(F32)).astype(BF16)
    return high, middle, low


def place():
    return lax.axis_index("ta"), lax.axis_index("ha")


def pack_kernel(plan_hbm, rows_hbm, out_ref, plan_ref, rows_ref, plan_sem, rows_sem):
    plan_copy = pltpu.make_async_copy(plan_hbm, plan_ref, plan_sem)
    rows_copy = pltpu.make_async_copy(rows_hbm, rows_ref, rows_sem)
    plan_copy.start()
    rows_copy.start()
    ta, ha = place()
    own = ta * 4 + ha
    lower = (iota((128, 128), 0) < iota((128, 128), 1)).astype(BF16)
    spot = iota((256, 128), 0)
    spot = (spot >> 4) * CAP + (spot & 7)
    plan_copy.wait()
    ids = plan_ref[pl.ds(own // 2, 1), :]
    ids = jnp.where(own % 2 == 1, pltpu.roll(ids, 64, 1), ids)
    block = ids >> 8
    hit = iota((16, 128), 0) == block
    before = dot(hit.astype(BF16), lower)
    rank = jnp.sum(jnp.where(hit, before, 0.0), axis=0, keepdims=True)
    hot = (spot == block * CAP + rank.astype(I32)).astype(BF16)
    rows_copy.wait()
    out_ref[...] = dot(hot[:, :SLOTS], rows_ref[...]).astype(BF16)


def same_group(lanes, wrap):
    first, second = iota((lanes, lanes), 0), iota((lanes, lanes), 1)
    if wrap < lanes:
        first = jnp.where(first >= wrap, first - wrap, first)
        second = jnp.where(second >= wrap, second - wrap, second)
    return (twelfth(first) == twelfth(second)).astype(BF16)


def side_by_side(weight_ref, out_ref):
    for tap in range(9):
        for c in range(2):
            part = weight_ref[tap, c * OWN : c * OWN + PAIR, :].astype(F32)
            at = tap * WIDE + c * CH
            out_ref[at : at + CH, :] = part.T.astype(BF16)


def side_by_side_dense(weight_ref, out_ref):
    for tap in range(9):
        for c in range(2):
            out_ref[tap, :, c * CH : (c + 1) * CH] = weight_ref[tap, c * OWN : c * OWN + PAIR, :]


def prepare_kernel(
    plan_hbm, gain_hbm, bias_hbm, b1_hbm, g2_hbm, n2_hbm, b2_hbm, w1_hbm, w2_hbm,
    table_ref, wide_ref, own_ref, same_wide_ref, same_own_ref, select_ref, first_ref, second_ref,
    plan_ref, gain_ref, bias_ref, b1_ref, g2_ref, n2_ref, b2_ref, w1_ref, w2_ref, sems,
):
    pairs = (
        (plan_hbm, plan_ref), (w1_hbm, w1_ref), (w2_hbm, w2_ref), (gain_hbm, gain_ref), (bias_hbm, bias_ref),
        (b1_hbm, b1_ref), (g2_hbm, g2_ref), (n2_hbm, n2_ref), (b2_hbm, b2_ref),
    )
    copies = [pltpu.make_async_copy(source, to, sems.at[k]) for k, (source, to) in enumerate(pairs)]
    for copy in copies:
        copy.start()
    ta, ha = place()
    same_wide_ref[...] = same_group(CH, CH)
    same_own_ref[...] = same_group(PAIR, OWN)
    lane = iota((WIDE, PAIR), 1)
    source = ha * OWN + jnp.where(lane < OWN, CH + lane, lane - OWN)
    select_ref[...] = (iota((WIDE, PAIR), 0) == source).astype(BF16)
    copies[0].wait()
    plan = plan_ref[...]
    match = (plan >> 8) == ta
    i, j = iota((128, 128), 0), iota((128, 128), 1)
    before = dot(match.astype(BF16), ((i < j) & ((i >> 6) == (j >> 6))).astype(BF16))
    value = jnp.where(match, (plan & 255) + 1, 0).astype(F32)
    ranked = jnp.concatenate([jnp.where(before == k, value, 0.0) for k in range(CAP)], axis=0)
    half = ((iota((8, 128), 1) >> 6) == iota((8, 128), 0)).astype(BF16)
    held = dot_nt(half, ranked.astype(BF16))
    q, p = iota((256, 256), 0), iota((256, 256), 1)
    held = dot(held.astype(BF16), (q == (p & 7) * 32 + (p >> 3)).astype(BF16))
    want = (q + 1).astype(F32)
    table_ref[:, 0:256] = (held[0:1] == want).astype(BF16)
    table_ref[:, 256:512] = (held[1:2] == want).astype(BF16)
    for copy in copies[3:]:
        copy.wait()
    wide_ref[0:1] = gain_ref[...].reshape(1, CH)
    wide_ref[1:2] = bias_ref[...].reshape(1, CH)
    for k, ref in enumerate((b1_ref, g2_ref, n2_ref, b2_ref)):
        value = ref[...].reshape(1, CH)
        part = jnp.zeros((1, OWN), F32)
        for h in range(4):
            part = jnp.where(ha == h, value[:, h * OWN : (h + 1) * OWN], part)
        own_ref[k : k + 1] = jnp.concatenate([part, part], axis=1)
    copies[1].wait()
    side_by_side(w1_ref, first_ref)
    copies[2].wait()
    side_by_side_dense(w2_ref, second_ref)


def unpack_kernel(table_ref, packed_ref, out_ref, tail_ref):
    rows = dot(table_ref[...], packed_ref[...]).astype(BF16)
    out_ref[...] = rows
    tail_ref[...] = rows[BLOCK - 64 :]


def frame_stats(values, same):
    rows, lanes = values.shape
    pick = ((iota((16, rows), 1) >> 4) == iota((16, rows), 0)).astype(BF16)
    wide = values.astype(F32)
    square = wide * wide
    high = square.astype(BF16)
    low = (square - high.astype(F32)).astype(BF16)
    both = jnp.concatenate([dot(pick, values), dot(pick, high) + dot(pick, low)], axis=0)
    if lanes == WIDE:
        both = both[:, :CH] + both[:, CH:]
    total = dot(jnp.concatenate(three(both), axis=0), same)
    total = total[0:32] + total[32:64] + total[64:96]
    entries = ROWS * 2 * GROUP
    mean = total[0:16] / entries
    var = total[16:32] / entries - mean * mean
    return mean, lax.rsqrt(var + 1e-06)


def silu(v):
    return v / (1.0 + jnp.exp(-v))


def store_taps(taps_ref, at, act):
    row = iota((ROWS, WIDE), 0)
    taps_ref[0, at : at + ROWS, :] = jnp.where(row == 0, 0.0, pltpu.roll(act, 1, 0)).astype(BF16)
    taps_ref[1, at : at + ROWS, :] = act.astype(BF16)
    taps_ref[2, at : at + ROWS, :] = jnp.where(row == ROWS - 1, 0.0, pltpu.roll(act, ROWS - 1, 0)).astype(BF16)


def norm_first(rows_ref, wide_ref, same, taps_ref):
    gain, bias = wide_ref[0:1], wide_ref[1:2]
    mean, inverse = frame_stats(rows_ref[...], same)
    for f in range(rows_ref.shape[0] // ROWS):
        value = rows_ref[f * ROWS : (f + 1) * ROWS, :].astype(F32)
        m, s = mean[f : f + 1], inverse[f : f + 1]
        halves = [
            silu((value[:, c * CH : (c + 1) * CH] - m) * s * gain + bias) for c in range(2)
        ]
        store_taps(taps_ref, f * ROWS, jnp.concatenate(halves, axis=1))


def convolve(taps_ref, product, rows, first_frame, count_ref):
    totals = []
    for a in range(3):
        acc = None
        for b in range(3):
            part = product(taps_ref[b, a * ROWS : a * ROWS + rows, :], 3 * a + b)
            acc = part if acc is None else acc + part
        totals.append(acc)
    frame = first_frame + (iota((rows, 1), 0) >> 4)
    start = jnp.zeros((rows, 1), I32)
    end = jnp.int32(0)
    for v in range(VIDEOS):
        count = count_ref[v]
        end = end + count
        start = start + jnp.where(frame >= end, count, 0)
    total = totals[2]
    for a in range(2):
        total = total + totals[a] * jnp.where(frame - 2 + a >= start, 1.0, 0.0)
    return total


def with_first(weight_ref):
    return lambda values, tap: dot(values, weight_ref[tap * WIDE : (tap + 1) * WIDE, :])


def with_second(weight_ref):
    return lambda values, tap: dot_nt(values, weight_ref[tap])


def fold(values):
    half = values.shape[0] // 2
    rest = values[:, 128:]
    return jnp.concatenate([values[:, :128], jnp.concatenate([rest[:half], rest[half:]], axis=1)], axis=0)


def norm_second(hidden, own_ref, same):
    gain, bias = own_ref[1:2], own_ref[2:3]
    mean, inverse = frame_stats(hidden, same)
    acts = []
    for f in range(hidden.shape[0] // ROWS):
        value = hidden[f * ROWS : (f + 1) * ROWS].astype(F32)
        acts.append(silu((value - mean[f : f + 1]) * inverse[f : f + 1] * gain + bias))
    return fold(jnp.concatenate(acts, axis=0)).astype(BF16)


EDGE = 64
INNER = BLOCK - 2 * ROWS
FOLDED = (EDGE + INNER) * 3 // 2
CUT = EDGE * 3 // 2


def main_kernel(
    count_ref, rows_ref, wide_ref, own_ref, same_wide_ref, same_own_ref, select_ref, weight_hbm,
    act_ref, rest_ref, head_ref, weight_ref, taps_ref, sem,
):
    copy = pltpu.make_async_copy(weight_hbm, weight_ref, sem)
    copy.start()
    ta, _ = place()
    norm_first(rows_ref, wide_ref, same_wide_ref[...], taps_ref)
    rest_ref[...] = dot(rows_ref[...], select_ref[...]).astype(BF16)
    for b in range(3):
        head_ref[b] = taps_ref[b, 0:32, :]
    copy.wait()
    hidden = convolve(taps_ref, with_first(weight_ref), INNER, ta * F_DEV + 2, count_ref) + own_ref[0:1]
    act_ref[...] = norm_second(hidden.astype(BF16), own_ref, same_own_ref[...])


def halo_kernel(
    count_ref, earlier_ref, head_ref, wide_ref, own_ref, same_wide_ref, same_own_ref, weight_ref, main_ref,
    act_ref, taps_ref,
):
    ta, _ = place()
    norm_first(earlier_ref, wide_ref, same_wide_ref[...], taps_ref)
    for b in range(3):
        taps_ref[b, EDGE : EDGE + 32, :] = head_ref[b]
    hidden = convolve(taps_ref, with_first(weight_ref), EDGE, ta * F_DEV - 2, count_ref) + own_ref[0:1]
    act_ref[0:CUT, :] = norm_second(hidden.astype(BF16), own_ref, same_own_ref[...])
    act_ref[CUT:FOLDED, :] = main_ref[...]


def unfolded(ref, h, base, frames, f):
    half = frames // 2
    low = base + frames * ROWS + (f % half) * ROWS
    lane = 64 * (f // half)
    return jnp.concatenate(
        [
            ref[h, base + f * ROWS : base + (f + 1) * ROWS, :].astype(F32),
            ref[h, low : low + ROWS, :].astype(F32)[:, lane : lane + 64],
        ],
        axis=1,
    )


def last_kernel(count_ref, act_ref, rest_ref, own_ref, weight_ref, out_ref, taps_ref):
    ta, _ = place()
    for f in range(F_DEV + 2):
        parts = [
            unfolded(act_ref, h, 0, 4, f) if f < 4 else unfolded(act_ref, h, CUT, 14, f - 4) for h in range(4)
        ]
        whole = jnp.concatenate([p[:, OWN:] for p in parts] + [p[:, :OWN] for p in parts], axis=1)
        store_taps(taps_ref, f * ROWS, whole)
    total = convolve(taps_ref, with_second(weight_ref), BLOCK, ta * F_DEV, count_ref)
    total = (total + own_ref[3:4] + rest_ref[...].astype(F32)).astype(BF16)
    to, at = iota((BLOCK, BLOCK), 0), iota((BLOCK, BLOCK), 1)
    order = (((to >> 2) & 15) * ROWS + (to >> 6) * 4 + (to & 3) == at).astype(BF16)
    ordered = dot(order, total)
    for h in range(4):
        out_ref[h] = fold(ordered[h * 64 : (h + 1) * 64]).astype(BF16)


def join_kernel(parts_ref, out_ref):
    parts = []
    for h in range(4):
        part = parts_ref[h].astype(F32)
        rest = jnp.concatenate([part[64:96, 0:64], part[64:96, 64:128]], axis=0)
        parts.append(jnp.concatenate([part[0:64], rest], axis=1))
    zero = jnp.concatenate([p[:, OWN:] for p in parts], axis=1)
    one = jnp.concatenate([p[:, :OWN] for p in parts], axis=1)
    out_ref[...] = jnp.stack([zero, one], axis=1).astype(BF16).reshape(F_DEV, 4, 2, CH)


def call(kernel, outs, ins, scratch=(), flops=0):
    run = pl.pallas_call(
        kernel,
        out_shape=[jax.ShapeDtypeStruct(*o) if isinstance(o, tuple) else o for o in outs],
        in_specs=[pl.BlockSpec(memory_space=m) for m in ins],
        out_specs=[pl.BlockSpec(memory_space=pltpu.VMEM)] * len(outs),
        scratch_shapes=list(scratch),
        compiler_params=pltpu.CompilerParams(vmem_limit_bytes=VMEM_LIMIT),
        cost_estimate=pl.CostEstimate(flops=flops, bytes_accessed=2**20, transcendentals=0),
    )

    def pinned(*args):
        return run(
            *(pltpu.with_memory_space_constraint(a, pltpu.HBM) if m is pltpu.HBM else a for a, m in zip(args, ins))
        )

    return pinned


def local(
    decoder_feature_rows,
    slot_row_index,
    latent_frame_count,
    first_norm_gain,
    first_norm_bias,
    first_convolution_weight,
    first_convolution_bias,
    second_norm_gain,
    second_norm_bias,
    second_convolution_weight,
    second_convolution_bias,
):
    plan = slot_row_index.reshape(32, 128)
    n_ta = lax.axis_size("ta")
    same_core = [[t * 4 + z * 2 + c for t in range(n_ta) for z in range(2)] for c in range(2)]
    chips = [[0, 1], [2, 3]]
    vmem, smem, hbm = pltpu.VMEM, pltpu.SMEM, pltpu.HBM

    [packed] = call(
        pack_kernel,
        [((256, WIDE), BF16)],
        [hbm] * 2,
        [pltpu.VMEM((32, 128), I32), pltpu.VMEM((SLOTS, WIDE), BF16)] + [pltpu.SemaphoreType.DMA] * 2,
        flops=10**7,
    )(plan, decoder_feature_rows)
    arrived = lax.all_to_all(
        packed.reshape(32, CAP, WIDE), ("ta", "ha"), 0, 0, axis_index_groups=same_core, tiled=True
    ).reshape(256, WIDE)
    weight, raw = (9 * WIDE, PAIR), (9, 3 * OWN, CH)
    table, wide, own, same_wide, same_own, select, first, second = call(
        prepare_kernel,
        [
            vmem((BLOCK, 512), BF16),
            vmem((2, CH), F32),
            vmem((4, PAIR), F32),
            vmem((CH, CH), BF16),
            vmem((PAIR, PAIR), BF16),
            vmem((WIDE, PAIR), BF16),
            hbm(weight, BF16),
            hbm((9, PAIR, WIDE), BF16),
        ],
        [hbm] * 9,
        [vmem((32, 128), I32)] + [vmem((CH,), F32)] * 6 + [vmem(raw, BF16)] * 2 + [pltpu.SemaphoreType.DMA((9,))],
        flops=2 * 10**9,
    )(
        plan,
        first_norm_gain,
        first_norm_bias,
        first_convolution_bias,
        second_norm_gain,
        second_norm_bias,
        second_convolution_bias,
        first_convolution_weight.reshape(raw),
        second_convolution_weight.reshape(raw),
    )
    both = lax.all_gather(arrived, "ha", axis=0, axis_index_groups=chips, tiled=True)
    rows, tail = call(unpack_kernel, [((BLOCK, WIDE), BF16), ((64, WIDE), BF16)], [vmem] * 2, flops=10**8)(table, both)
    earlier = lax.ppermute(tail, "ta", [(i, i + 1) for i in range(n_ta - 1)])
    act, rest, head, near = call(
        main_kernel,
        [
            vmem((FOLDED - CUT, 128), BF16),
            vmem((BLOCK, PAIR), BF16),
            vmem((3, 32, WIDE), BF16),
            vmem(weight, BF16),
        ],
        [smem] + [vmem] * 6 + [hbm],
        [vmem((3, BLOCK, WIDE), BF16), pltpu.SemaphoreType.DMA],
        flops=2 * 10**9,
    )(latent_frame_count, rows, wide, own, same_wide, same_own, select, first)
    [act] = call(
        halo_kernel, [((FOLDED, 128), BF16)], [smem] + [vmem] * 8, [vmem((3, EDGE + 32, WIDE), BF16)], flops=10**9
    )(latent_frame_count, earlier, head, wide, own, same_wide, same_own, near, act)
    acts = lax.all_gather(act, "ha", axis=0, tiled=False)
    [out] = call(
        last_kernel,
        [((4, 96, 128), BF16)],
        [smem] + [vmem] * 4,
        [pltpu.VMEM((3, EDGE + INNER, WIDE), BF16)],
        flops=2 * 10**9,
    )(latent_frame_count, acts, rest, own, second)
    parts = lax.all_to_all(out, "ha", 0, 0, tiled=True)
    [joined] = call(join_kernel, [((F_DEV, 4, 2, CH), BF16)], [vmem])(parts)
    return joined


def solution(mesh):
    in_specs = (
        P(("dp", "ta", "ha"), None),
        P("dp"),
        P("dp"),
        P(),
        P(),
        P(None, None, None, "ha", None),
        P(),
        P(),
        P(),
        P(None, None, None, "ha", None),
        P(),
    )
    out_specs = P(("dp", "ta"), "ha", None, None)
    return jax.shard_map(local, mesh=mesh, in_specs=in_specs, out_specs=out_specs, check_vma=False)
```

```python
import jax
import jax.numpy as jnp
from jax import lax
from jax.experimental import pallas as pl
from jax.experimental.pallas import tpu as pltpu
from jax.sharding import PartitionSpec as P

CH = 384
WIDE = 768
GROUP = 12
ROWS = 16
OWN = 96
PAIR = 192
F_DEV = 16
BLOCK = 256
SLOTS = 64
CAP = 8
VIDEOS = 6
F32, BF16, I32 = jnp.float32, jnp.bfloat16, jnp.int32
VMEM_LIMIT = 24 * 2**20


def dot(a, b):
    return jnp.dot(a, b, preferred_element_type=F32)


def dot_nt(a, b):
    return lax.dot_general(a, b, (((1,), (1,)), ((), ())), preferred_element_type=F32)


def iota(shape, axis):
    return lax.broadcasted_iota(I32, shape, axis)


def twelfth(v):
    return (v * 43691) >> 19


def three(v):
    high = v.astype(BF16)
    rest = v - high.astype(F32)
    middle = rest.astype(BF16)
    low = (rest - middle.astype(F32)).astype(BF16)
    return high, middle, low


def place():
    return lax.axis_index("ta"), lax.axis_index("ha")


def pack_kernel(plan_hbm, rows_hbm, out_ref, plan_ref, rows_ref, plan_sem, rows_sem):
    plan_copy = pltpu.make_async_copy(plan_hbm, plan_ref, plan_sem)
    rows_copy = pltpu.make_async_copy(rows_hbm, rows_ref, rows_sem)
    plan_copy.start()
    rows_copy.start()
    ta, ha = place()
    own = ta * 4 + ha
    lower = (iota((128, 128), 0) < iota((128, 128), 1)).astype(BF16)
    spot = iota((256, 128), 0)
    spot = (spot >> 4) * CAP + (spot & 7)
    plan_copy.wait()
    ids = plan_ref[pl.ds(own // 2, 1), :]
    ids = jnp.where(own % 2 == 1, pltpu.roll(ids, 64, 1), ids)
    block = ids >> 8
    hit = iota((16, 128), 0) == block
    before = dot(hit.astype(BF16), lower)
    rank = jnp.sum(jnp.where(hit, before, 0.0), axis=0, keepdims=True)
    hot = (spot == block * CAP + rank.astype(I32)).astype(BF16)
    rows_copy.wait()
    out_ref[...] = dot(hot[:, :SLOTS], rows_ref[...]).astype(BF16)


def same_group(lanes, wrap):
    first, second = iota((lanes, lanes), 0), iota((lanes, lanes), 1)
    if wrap < lanes:
        first = jnp.where(first >= wrap, first - wrap, first)
        second = jnp.where(second >= wrap, second - wrap, second)
    return (twelfth(first) == twelfth(second)).astype(BF16)


def side_by_side(weight_ref, out_ref):
    for tap in range(9):
        for c in range(2):
            out_ref[tap, :, c * CH : (c + 1) * CH] = weight_ref[tap, c * OWN : c * OWN + PAIR, :]


def prepare_kernel(
    plan_hbm, gain_hbm, bias_hbm, b1_hbm, g2_hbm, n2_hbm, b2_hbm, w2_hbm,
    table_ref, wide_ref, own_ref, same_wide_ref, same_own_ref, select_ref, second_ref,
    plan_ref, gain_ref, bias_ref, b1_ref, g2_ref, n2_ref, b2_ref, w2_ref, sems,
):
    pairs = (
        (plan_hbm, plan_ref), (w2_hbm, w2_ref), (gain_hbm, gain_ref), (bias_hbm, bias_ref),
        (b1_hbm, b1_ref), (g2_hbm, g2_ref), (n2_hbm, n2_ref), (b2_hbm, b2_ref),
    )
    copies = [pltpu.make_async_copy(source, to, sems.at[k]) for k, (source, to) in enumerate(pairs)]
    for copy in copies:
        copy.start()
    ta, ha = place()
    same_wide_ref[...] = same_group(CH, CH)
    same_own_ref[...] = same_group(PAIR, OWN)
    lane = iota((WIDE, PAIR), 1)
    source = ha * OWN + jnp.where(lane < OWN, CH + lane, lane - OWN)
    select_ref[...] = (iota((WIDE, PAIR), 0) == source).astype(BF16)
    copies[0].wait()
    plan = plan_ref[...]
    match = (plan >> 8) == ta
    i, j = iota((128, 128), 0), iota((128, 128), 1)
    before = dot(match.astype(BF16), ((i < j) & ((i >> 6) == (j >> 6))).astype(BF16))
    value = jnp.where(match, (plan & 255) + 1, 0).astype(F32)
    ranked = jnp.concatenate([jnp.where(before == k, value, 0.0) for k in range(CAP)], axis=0)
    half = ((iota((8, 128), 1) >> 6) == iota((8, 128), 0)).astype(BF16)
    held = dot_nt(half, ranked.astype(BF16))
    q, p = iota((256, 256), 0), iota((256, 256), 1)
    held = dot(held.astype(BF16), (q == (p & 7) * 32 + (p >> 3)).astype(BF16))
    want = (q + 1).astype(F32)
    table_ref[:, 0:256] = (held[0:1] == want).astype(BF16)
    table_ref[:, 256:512] = (held[1:2] == want).astype(BF16)
    for copy in copies[2:]:
        copy.wait()
    wide_ref[0:1] = gain_ref[...].reshape(1, CH)
    wide_ref[1:2] = bias_ref[...].reshape(1, CH)
    for k, ref in enumerate((b1_ref, g2_ref, n2_ref, b2_ref)):
        value = ref[...].reshape(1, CH)
        part = jnp.zeros((1, OWN), F32)
        for h in range(4):
            part = jnp.where(ha == h, value[:, h * OWN : (h + 1) * OWN], part)
        own_ref[k : k + 1] = jnp.concatenate([part, part], axis=1)
    copies[1].wait()
    side_by_side(w2_ref, second_ref)


def tail_kernel(table_ref, packed_ref, tail_ref):
    tail_ref[...] = dot(table_ref[BLOCK - EDGE :, :], packed_ref[...]).astype(BF16)


def frame_stats(values, same):
    rows, lanes = values.shape
    pick = ((iota((16, rows), 1) >> 4) == iota((16, rows), 0)).astype(BF16)
    wide = values.astype(F32)
    square = wide * wide
    high = square.astype(BF16)
    low = (square - high.astype(F32)).astype(BF16)
    both = jnp.concatenate([dot(pick, values), dot(pick, high) + dot(pick, low)], axis=0)
    if lanes == WIDE:
        both = both[:, :CH] + both[:, CH:]
    total = dot(jnp.concatenate(three(both), axis=0), same)
    total = total[0:32] + total[32:64] + total[64:96]
    entries = ROWS * 2 * GROUP
    mean = total[0:16] / entries
    var = total[16:32] / entries - mean * mean
    return mean, lax.rsqrt(var + 1e-06)


def silu(v):
    return v / (1.0 + jnp.exp(-v))


def store_taps(taps_ref, at, act):
    row = iota((ROWS, WIDE), 0)
    taps_ref[0, at : at + ROWS, :] = jnp.where(row == 0, 0.0, pltpu.roll(act, 1, 0)).astype(BF16)
    taps_ref[1, at : at + ROWS, :] = act.astype(BF16)
    taps_ref[2, at : at + ROWS, :] = jnp.where(row == ROWS - 1, 0.0, pltpu.roll(act, ROWS - 1, 0)).astype(BF16)


def norm_first(rows_ref, wide_ref, same, taps_ref):
    gain, bias = wide_ref[0:1], wide_ref[1:2]
    mean, inverse = frame_stats(rows_ref[...], same)
    for f in range(rows_ref.shape[0] // ROWS):
        value = rows_ref[f * ROWS : (f + 1) * ROWS, :].astype(F32)
        m, s = mean[f : f + 1], inverse[f : f + 1]
        halves = [
            silu((value[:, c * CH : (c + 1) * CH] - m) * s * gain + bias) for c in range(2)
        ]
        store_taps(taps_ref, f * ROWS, jnp.concatenate(halves, axis=1))


def convolve(taps_ref, product, rows, first_frame, count_ref):
    totals = []
    for a in range(3):
        acc = None
        for b in range(3):
            part = product(taps_ref[b, a * ROWS : a * ROWS + rows, :], 3 * a + b)
            acc = part if acc is None else acc + part
        totals.append(acc)
    frame = first_frame + (iota((rows, 1), 0) >> 4)
    start = jnp.zeros((rows, 1), I32)
    end = jnp.int32(0)
    for v in range(VIDEOS):
        count = count_ref[v]
        end = end + count
        start = start + jnp.where(frame >= end, count, 0)
    total = totals[2]
    for a in range(2):
        total = total + totals[a] * jnp.where(frame - 2 + a >= start, 1.0, 0.0)
    return total


def with_weights(weight_ref):
    return lambda values, tap: dot_nt(values, weight_ref[tap])


def fold(values):
    half = values.shape[0] // 2
    rest = values[:, 128:]
    return jnp.concatenate([values[:, :128], jnp.concatenate([rest[:half], rest[half:]], axis=1)], axis=0)


def norm_second(hidden, own_ref, same):
    gain, bias = own_ref[1:2], own_ref[2:3]
    mean, inverse = frame_stats(hidden, same)
    acts = []
    for f in range(hidden.shape[0] // ROWS):
        value = hidden[f * ROWS : (f + 1) * ROWS].astype(F32)
        acts.append(silu((value - mean[f : f + 1]) * inverse[f : f + 1] * gain + bias))
    return fold(jnp.concatenate(acts, axis=0)).astype(BF16)


EDGE = 64
INNER = BLOCK - 2 * ROWS
FOLDED = (EDGE + INNER) * 3 // 2
CUT = EDGE * 3 // 2


def main_kernel(
    count_ref, table_ref, packed_ref, wide_ref, own_ref, same_wide_ref, same_own_ref, select_ref, raw_ref,
    act_ref, rest_ref, head_ref, weight_ref, rows_ref, taps_ref,
):
    ta, _ = place()
    rows_ref[...] = dot(table_ref[...], packed_ref[...]).astype(BF16)
    side_by_side(raw_ref, weight_ref)
    norm_first(rows_ref, wide_ref, same_wide_ref[...], taps_ref)
    rest_ref[...] = dot(rows_ref[...], select_ref[...]).astype(BF16)
    for b in range(3):
        head_ref[b] = taps_ref[b, 0:32, :]
    hidden = convolve(taps_ref, with_weights(weight_ref), INNER, ta * F_DEV + 2, count_ref) + own_ref[0:1]
    act_ref[...] = norm_second(hidden.astype(BF16), own_ref, same_own_ref[...])


def halo_kernel(
    count_ref, earlier_ref, head_ref, wide_ref, own_ref, same_wide_ref, same_own_ref, weight_ref, main_ref,
    act_ref, taps_ref,
):
    ta, _ = place()
    norm_first(earlier_ref, wide_ref, same_wide_ref[...], taps_ref)
    for b in range(3):
        taps_ref[b, EDGE : EDGE + 32, :] = head_ref[b]
    hidden = convolve(taps_ref, with_weights(weight_ref), EDGE, ta * F_DEV - 2, count_ref) + own_ref[0:1]
    act_ref[0:CUT, :] = norm_second(hidden.astype(BF16), own_ref, same_own_ref[...])
    act_ref[CUT:FOLDED, :] = main_ref[...]


def unfolded(ref, h, base, frames, f):
    half = frames // 2
    low = base + frames * ROWS + (f % half) * ROWS
    lane = 64 * (f // half)
    return jnp.concatenate(
        [
            ref[h, base + f * ROWS : base + (f + 1) * ROWS, :].astype(F32),
            ref[h, low : low + ROWS, :].astype(F32)[:, lane : lane + 64],
        ],
        axis=1,
    )


def last_kernel(count_ref, act_ref, rest_ref, own_ref, weight_ref, out_ref, taps_ref):
    ta, _ = place()
    for f in range(F_DEV + 2):
        parts = [
            unfolded(act_ref, h, 0, 4, f) if f < 4 else unfolded(act_ref, h, CUT, 14, f - 4) for h in range(4)
        ]
        whole = jnp.concatenate([p[:, OWN:] for p in parts] + [p[:, :OWN] for p in parts], axis=1)
        store_taps(taps_ref, f * ROWS, whole)
    total = convolve(taps_ref, with_weights(weight_ref), BLOCK, ta * F_DEV, count_ref)
    total = (total + own_ref[3:4] + rest_ref[...].astype(F32)).astype(BF16)
    to, at = iota((BLOCK, BLOCK), 0), iota((BLOCK, BLOCK), 1)
    order = (((to >> 2) & 15) * ROWS + (to >> 6) * 4 + (to & 3) == at).astype(BF16)
    ordered = dot(order, total)
    for h in range(4):
        out_ref[h] = fold(ordered[h * 64 : (h + 1) * 64]).astype(BF16)


def join_kernel(parts_ref, out_ref):
    parts = []
    for h in range(4):
        part = parts_ref[h].astype(F32)
        rest = jnp.concatenate([part[64:96, 0:64], part[64:96, 64:128]], axis=0)
        parts.append(jnp.concatenate([part[0:64], rest], axis=1))
    zero = jnp.concatenate([p[:, OWN:] for p in parts], axis=1)
    one = jnp.concatenate([p[:, :OWN] for p in parts], axis=1)
    out_ref[...] = jnp.stack([zero, one], axis=1).astype(BF16).reshape(F_DEV, 4, 2, CH)


def call(kernel, outs, ins, scratch=(), flops=0):
    run = pl.pallas_call(
        kernel,
        out_shape=[jax.ShapeDtypeStruct(*o) if isinstance(o, tuple) else o for o in outs],
        in_specs=[pl.BlockSpec(memory_space=m) for m in ins],
        out_specs=[pl.BlockSpec(memory_space=pltpu.VMEM)] * len(outs),
        scratch_shapes=list(scratch),
        compiler_params=pltpu.CompilerParams(vmem_limit_bytes=VMEM_LIMIT),
        cost_estimate=pl.CostEstimate(flops=flops, bytes_accessed=2**20, transcendentals=0),
    )

    def pinned(*args):
        return run(
            *(pltpu.with_memory_space_constraint(a, pltpu.HBM) if m is pltpu.HBM else a for a, m in zip(args, ins))
        )

    return pinned


def local(
    decoder_feature_rows,
    slot_row_index,
    latent_frame_count,
    first_norm_gain,
    first_norm_bias,
    first_convolution_weight,
    first_convolution_bias,
    second_norm_gain,
    second_norm_bias,
    second_convolution_weight,
    second_convolution_bias,
):
    plan = slot_row_index.reshape(32, 128)
    n_ta = lax.axis_size("ta")
    same_core = [[t * 4 + z * 2 + c for t in range(n_ta) for z in range(2)] for c in range(2)]
    chips = [[0, 1], [2, 3]]
    vmem, smem, hbm = pltpu.VMEM, pltpu.SMEM, pltpu.HBM

    [packed] = call(
        pack_kernel,
        [vmem((256, WIDE), BF16)],
        [hbm] * 2,
        [pltpu.VMEM((32, 128), I32), pltpu.VMEM((SLOTS, WIDE), BF16)] + [pltpu.SemaphoreType.DMA] * 2,
        flops=10**7,
    )(plan, decoder_feature_rows)
    arrived = lax.all_to_all(
        packed.reshape(32, CAP, WIDE), ("ta", "ha"), 0, 0, axis_index_groups=same_core, tiled=True
    ).reshape(256, WIDE)
    weight, raw = (9, PAIR, WIDE), (9, 3 * OWN, CH)
    table, wide, own, same_wide, same_own, select, second = call(
        prepare_kernel,
        [
            vmem((BLOCK, 512), BF16),
            vmem((2, CH), F32),
            vmem((4, PAIR), F32),
            vmem((CH, CH), BF16),
            vmem((PAIR, PAIR), BF16),
            vmem((WIDE, PAIR), BF16),
            hbm(weight, BF16),
        ],
        [hbm] * 8,
        [vmem((32, 128), I32)] + [vmem((CH,), F32)] * 6 + [vmem(raw, BF16), pltpu.SemaphoreType.DMA((8,))],
        flops=2 * 10**9,
    )(
        plan,
        first_norm_gain,
        first_norm_bias,
        first_convolution_bias,
        second_norm_gain,
        second_norm_bias,
        second_convolution_bias,
        second_convolution_weight.reshape(raw),
    )
    both = lax.all_gather(arrived, "ha", axis=0, axis_index_groups=chips, tiled=True)
    [tail] = call(tail_kernel, [((EDGE, WIDE), BF16)], [vmem] * 2, flops=10**8)(table, both)
    earlier = lax.ppermute(tail, "ta", [(i, i + 1) for i in range(n_ta - 1)])
    act, rest, head, near = call(
        main_kernel,
        [
            vmem((FOLDED - CUT, 128), BF16),
            vmem((BLOCK, PAIR), BF16),
            vmem((3, 32, WIDE), BF16),
            vmem(weight, BF16),
        ],
        [smem] + [vmem] * 8,
        [vmem((BLOCK, WIDE), BF16), vmem((3, BLOCK, WIDE), BF16)],
        flops=2 * 10**9,
    )(latent_frame_count, table, both, wide, own, same_wide, same_own, select, first_convolution_weight.reshape(raw))
    [act] = call(
        halo_kernel, [((FOLDED, 128), BF16)], [smem] + [vmem] * 8, [vmem((3, EDGE + 32, WIDE), BF16)], flops=10**9
    )(latent_frame_count, earlier, head, wide, own, same_wide, same_own, near, act)
    acts = lax.all_gather(act, "ha", axis=0, tiled=False)
    [out] = call(
        last_kernel,
        [((4, 96, 128), BF16)],
        [smem] + [vmem] * 4,
        [pltpu.VMEM((3, EDGE + INNER, WIDE), BF16)],
        flops=2 * 10**9,
    )(latent_frame_count, acts, rest, own, second)
    parts = lax.all_to_all(out, "ha", 0, 0, tiled=True)
    [joined] = call(join_kernel, [((F_DEV, 4, 2, CH), BF16)], [vmem])(parts)
    return joined


def solution(mesh):
    in_specs = (
        P(("dp", "ta", "ha"), None),
        P("dp"),
        P("dp"),
        P(),
        P(),
        P(None, None, None, "ha", None),
        P(),
        P(),
        P(),
        P(None, None, None, "ha", None),
        P(),
    )
    out_specs = P(("dp", "ta"), "ha", None, None)
    return jax.shard_map(local, mesh=mesh, in_specs=in_specs, out_specs=out_specs, check_vma=False)
```

```python
import jax
import jax.numpy as jnp
from jax import lax
from jax.experimental import pallas as pl
from jax.experimental.pallas import tpu as pltpu
from jax.sharding import PartitionSpec as P

CH = 384
WIDE = 768
GROUP = 12
ROWS = 16
OWN = 96
PAIR = 192
F_DEV = 16
BLOCK = 256
SLOTS = 64
CAP = 8
VIDEOS = 6
EDGE = 64
INNER = BLOCK - 2 * ROWS
FOLDED = (EDGE + INNER) * 3 // 2
CUT = EDGE * 3 // 2
F32, BF16, I32 = jnp.float32, jnp.bfloat16, jnp.int32
VMEM_LIMIT = 24 * 2**20


def dot(a, b):
    return jnp.dot(a, b, preferred_element_type=F32)


def dot_nt(a, b):
    return lax.dot_general(a, b, (((1,), (1,)), ((), ())), preferred_element_type=F32)


def iota(shape, axis):
    return lax.broadcasted_iota(I32, shape, axis)


def twelfth(v):
    return (v * 43691) >> 19


def three(v):
    high = v.astype(BF16)
    rest = v - high.astype(F32)
    middle = rest.astype(BF16)
    low = (rest - middle.astype(F32)).astype(BF16)
    return high, middle, low


def place():
    return lax.axis_index("ta"), lax.axis_index("ha")


def pack_kernel(plan_hbm, rows_hbm, out_ref, plan_ref, rows_ref, plan_sem, rows_sem):
    plan_copy = pltpu.make_async_copy(plan_hbm, plan_ref, plan_sem)
    rows_copy = pltpu.make_async_copy(rows_hbm, rows_ref, rows_sem)
    plan_copy.start()
    rows_copy.start()
    ta, ha = place()
    own = ta * 4 + ha
    lower = (iota((128, 128), 0) < iota((128, 128), 1)).astype(BF16)
    spot = iota((256, 128), 0)
    spot = (spot >> 4) * CAP + (spot & 7)
    plan_copy.wait()
    ids = plan_ref[pl.ds(own // 2, 1), :]
    ids = jnp.where(own % 2 == 1, pltpu.roll(ids, 64, 1), ids)
    block = ids >> 8
    hit = iota((16, 128), 0) == block
    before = dot(hit.astype(BF16), lower)
    rank = jnp.sum(jnp.where(hit, before, 0.0), axis=0, keepdims=True)
    hot = (spot == block * CAP + rank.astype(I32)).astype(BF16)
    rows_copy.wait()
    out_ref[...] = dot(hot[:, :SLOTS], rows_ref[...]).astype(BF16)


def same_group(lanes, wrap):
    first, second = iota((lanes, lanes), 0), iota((lanes, lanes), 1)
    if wrap < lanes:
        first = jnp.where(first >= wrap, first - wrap, first)
        second = jnp.where(second >= wrap, second - wrap, second)
    return (twelfth(first) == twelfth(second)).astype(BF16)


def side_by_side(weight_ref, out_ref):
    for tap in range(9):
        for c in range(2):
            out_ref[tap, :, c * CH : (c + 1) * CH] = weight_ref[tap, c * OWN : c * OWN + PAIR, :]


def prepare_kernel(
    count_ref, plan_hbm, gain_hbm, bias_hbm, b1_hbm, g2_hbm, n2_hbm, b2_hbm, w2_hbm,
    table_ref, keep_ref, wide_ref, own_ref, same_wide_ref, same_own_ref, select_ref, second_ref,
    plan_ref, gain_ref, bias_ref, b1_ref, g2_ref, n2_ref, b2_ref, w2_ref, sems,
):
    pairs = (
        (plan_hbm, plan_ref), (w2_hbm, w2_ref), (gain_hbm, gain_ref), (bias_hbm, bias_ref),
        (b1_hbm, b1_ref), (g2_hbm, g2_ref), (n2_hbm, n2_ref), (b2_hbm, b2_ref),
    )
    copies = [pltpu.make_async_copy(source, to, sems.at[k]) for k, (source, to) in enumerate(pairs)]
    for copy in copies:
        copy.start()
    ta, ha = place()
    frame = ta * F_DEV - 2 + (iota((EDGE + INNER, 2), 0) >> 4)
    start = jnp.zeros((EDGE + INNER, 2), I32)
    end = jnp.int32(0)
    for v in range(VIDEOS):
        count = count_ref[v]
        end = end + count
        start = start + jnp.where(frame >= end, count, 0)
    keep_ref[...] = jnp.where(frame - 2 + iota((EDGE + INNER, 2), 1) >= start, 1.0, 0.0).astype(BF16)
    same_wide_ref[...] = same_group(CH, CH)
    same_own_ref[...] = same_group(PAIR, OWN)
    lane = iota((PAIR, WIDE), 0)
    source = ha * OWN + jnp.where(lane < OWN, CH + lane, lane - OWN)
    select_ref[...] = (iota((PAIR, WIDE), 1) == source).astype(BF16)
    copies[0].wait()
    plan = plan_ref[...]
    match = (plan >> 8) == ta
    i, j = iota((128, 128), 0), iota((128, 128), 1)
    before = dot(match.astype(BF16), ((i < j) & ((i >> 6) == (j >> 6))).astype(BF16))
    value = jnp.where(match, (plan & 255) + 1, 0).astype(F32)
    ranked = jnp.concatenate([jnp.where(before == k, value, 0.0) for k in range(CAP)], axis=0)
    half = ((iota((8, 128), 1) >> 6) == iota((8, 128), 0)).astype(BF16)
    held = dot_nt(half, ranked.astype(BF16))
    q, p = iota((256, 256), 0), iota((256, 256), 1)
    held = dot(held.astype(BF16), (q == (p & 7) * 32 + (p >> 3)).astype(BF16))
    want = (q + 1).astype(F32)
    table_ref[:, 0:256] = (held[0:1] == want).astype(BF16)
    table_ref[:, 256:512] = (held[1:2] == want).astype(BF16)
    for copy in copies[2:]:
        copy.wait()
    wide_ref[0:1] = gain_ref[...].reshape(1, CH)
    wide_ref[1:2] = bias_ref[...].reshape(1, CH)
    for k, ref in enumerate((b1_ref, g2_ref, n2_ref, b2_ref)):
        value = ref[...].reshape(1, CH)
        part = jnp.zeros((1, OWN), F32)
        for h in range(4):
            part = jnp.where(ha == h, value[:, h * OWN : (h + 1) * OWN], part)
        own_ref[k : k + 1] = jnp.concatenate([part, part], axis=1)
    copies[1].wait()
    side_by_side(w2_ref, second_ref)


def tail_kernel(table_ref, packed_ref, tail_ref):
    tail_ref[...] = dot(table_ref[BLOCK - EDGE :, :], packed_ref[...]).astype(BF16)


def squares(values):
    wide = values.astype(F32)
    square = wide * wide
    high = square.astype(BF16)
    return high, (square - high.astype(F32)).astype(BF16)


def moments(total, total_squares):
    entries = ROWS * 2 * GROUP
    mean = total / entries
    return mean, lax.rsqrt(total_squares / entries - mean * mean + 1e-06)


def wide_stats(values, same):
    rows = values.shape[0]
    pick = ((iota((16, rows), 1) >> 4) == iota((16, rows), 0)).astype(BF16)
    high, low = squares(values)
    both = jnp.concatenate([dot(pick, values), dot(pick, high) + dot(pick, low)], axis=0)
    both = both[:, :CH] + both[:, CH:]
    total = dot(jnp.concatenate(three(both), axis=0), same)
    total = total[0:32] + total[32:64] + total[64:96]
    return moments(total[0:16], total[16:32])


def own_stats(values, same):
    rows = values.shape[0]
    total = dot(jnp.concatenate([values, *squares(values)], axis=0), same)
    by_frame = [
        jnp.sum(part.reshape(rows // ROWS, ROWS, PAIR), axis=1)
        for part in (total[:rows], total[rows : 2 * rows] + total[2 * rows :])
    ]
    return moments(*by_frame)


def silu(v):
    return v / (1.0 + jnp.exp(-v))


def store_taps(taps_ref, at, act):
    row = iota((ROWS, WIDE), 0)
    taps_ref[0, at : at + ROWS, :] = jnp.where(row == 0, 0.0, pltpu.roll(act, 1, 0)).astype(BF16)
    taps_ref[1, at : at + ROWS, :] = act.astype(BF16)
    taps_ref[2, at : at + ROWS, :] = jnp.where(row == ROWS - 1, 0.0, pltpu.roll(act, ROWS - 1, 0)).astype(BF16)


def norm_first(rows_ref, wide_ref, same, taps_ref):
    gain, bias = wide_ref[0:1], wide_ref[1:2]
    mean, inverse = wide_stats(rows_ref[...], same)
    for f in range(rows_ref.shape[0] // ROWS):
        value = rows_ref[f * ROWS : (f + 1) * ROWS, :].astype(F32)
        m, s = mean[f : f + 1], inverse[f : f + 1]
        halves = [
            silu((value[:, c * CH : (c + 1) * CH] - m) * s * gain + bias) for c in range(2)
        ]
        store_taps(taps_ref, f * ROWS, jnp.concatenate(halves, axis=1))


def convolve(taps_ref, product, rows, keep):
    totals = []
    for a in range(3):
        acc = None
        for b in range(3):
            part = product(taps_ref[b, a * ROWS : a * ROWS + rows, :], 3 * a + b)
            acc = part if acc is None else acc + part
        totals.append(acc)
    keep = keep.astype(F32)
    return totals[2] + totals[0] * keep[:, 0:1] + totals[1] * keep[:, 1:2]


def with_weights(weight_ref):
    return lambda values, tap: dot_nt(values, weight_ref[tap])


def fold(values):
    half = values.shape[0] // 2
    rest = values[:, 128:]
    return jnp.concatenate([values[:, :128], jnp.concatenate([rest[:half], rest[half:]], axis=1)], axis=0)


def norm_second(hidden, own_ref, same):
    gain, bias = own_ref[1:2], own_ref[2:3]
    mean, inverse = own_stats(hidden, same)
    acts = []
    for f in range(hidden.shape[0] // ROWS):
        value = hidden[f * ROWS : (f + 1) * ROWS].astype(F32)
        acts.append(silu((value - mean[f : f + 1]) * inverse[f : f + 1] * gain + bias))
    return fold(jnp.concatenate(acts, axis=0)).astype(BF16)


def main_kernel(
    keep_ref, table_ref, packed_ref, wide_ref, own_ref, same_wide_ref, same_own_ref, select_ref, raw_ref,
    act_ref, rest_ref, head_ref, weight_ref, rows_ref, taps_ref,
):
    rows_ref[...] = dot(table_ref[...], packed_ref[...]).astype(BF16)
    side_by_side(raw_ref, weight_ref)
    norm_first(rows_ref, wide_ref, same_wide_ref[...], taps_ref)
    rest_ref[...] = dot_nt(rows_ref[...], select_ref[...]).astype(BF16)
    for b in range(3):
        head_ref[b] = taps_ref[b, 0:32, :]
    hidden = convolve(taps_ref, with_weights(weight_ref), INNER, keep_ref[EDGE:, :]) + own_ref[0:1]
    act_ref[...] = norm_second(hidden.astype(BF16), own_ref, same_own_ref[...])


def halo_kernel(
    keep_ref, earlier_ref, head_ref, wide_ref, own_ref, same_wide_ref, same_own_ref, weight_ref, main_ref,
    act_ref, taps_ref,
):
    norm_first(earlier_ref, wide_ref, same_wide_ref[...], taps_ref)
    for b in range(3):
        taps_ref[b, EDGE : EDGE + 32, :] = head_ref[b]
    hidden = convolve(taps_ref, with_weights(weight_ref), EDGE, keep_ref[0:EDGE, :]) + own_ref[0:1]
    act_ref[0:CUT, :] = norm_second(hidden.astype(BF16), own_ref, same_own_ref[...])
    act_ref[CUT:FOLDED, :] = main_ref[...]


def unfolded(ref, h, base, frames, f):
    half = frames // 2
    low = base + frames * ROWS + (f % half) * ROWS
    lane = 64 * (f // half)
    return jnp.concatenate(
        [
            ref[h, base + f * ROWS : base + (f + 1) * ROWS, :].astype(F32),
            ref[h, low : low + ROWS, :].astype(F32)[:, lane : lane + 64],
        ],
        axis=1,
    )


def last_kernel(keep_ref, act_ref, rest_ref, own_ref, weight_ref, out_ref, taps_ref):
    for f in range(F_DEV + 2):
        parts = [
            unfolded(act_ref, h, 0, 4, f) if f < 4 else unfolded(act_ref, h, CUT, 14, f - 4) for h in range(4)
        ]
        whole = jnp.concatenate([p[:, OWN:] for p in parts] + [p[:, :OWN] for p in parts], axis=1)
        store_taps(taps_ref, f * ROWS, whole)
    total = convolve(taps_ref, with_weights(weight_ref), BLOCK, keep_ref[2 * ROWS :, :])
    total = (total + own_ref[3:4] + rest_ref[...].astype(F32)).astype(BF16)
    to, at = iota((BLOCK, BLOCK), 0), iota((BLOCK, BLOCK), 1)
    order = (((to >> 2) & 15) * ROWS + (to >> 6) * 4 + (to & 3) == at).astype(BF16)
    ordered = dot(order, total)
    for h in range(4):
        out_ref[h] = fold(ordered[h * 64 : (h + 1) * 64]).astype(BF16)


def join_kernel(parts_ref, out_ref):
    parts = []
    for h in range(4):
        part = parts_ref[h].astype(F32)
        rest = jnp.concatenate([part[64:96, 0:64], part[64:96, 64:128]], axis=0)
        parts.append(jnp.concatenate([part[0:64], rest], axis=1))
    zero = jnp.concatenate([p[:, OWN:] for p in parts], axis=1)
    one = jnp.concatenate([p[:, :OWN] for p in parts], axis=1)
    out_ref[...] = jnp.stack([zero, one], axis=1).astype(BF16).reshape(F_DEV, 4, 2, CH)


def call(kernel, outs, ins, scratch=(), flops=0):
    run = pl.pallas_call(
        kernel,
        out_shape=[jax.ShapeDtypeStruct(*o) if isinstance(o, tuple) else o for o in outs],
        in_specs=[pl.BlockSpec(memory_space=m) for m in ins],
        out_specs=[pl.BlockSpec(memory_space=pltpu.VMEM)] * len(outs),
        scratch_shapes=list(scratch),
        compiler_params=pltpu.CompilerParams(vmem_limit_bytes=VMEM_LIMIT),
        cost_estimate=pl.CostEstimate(flops=flops, bytes_accessed=2**20, transcendentals=0),
    )

    def pinned(*args):
        return run(
            *(pltpu.with_memory_space_constraint(a, pltpu.HBM) if m is pltpu.HBM else a for a, m in zip(args, ins))
        )

    return pinned


def local(
    decoder_feature_rows,
    slot_row_index,
    latent_frame_count,
    first_norm_gain,
    first_norm_bias,
    first_convolution_weight,
    first_convolution_bias,
    second_norm_gain,
    second_norm_bias,
    second_convolution_weight,
    second_convolution_bias,
):
    plan = slot_row_index.reshape(32, 128)
    n_ta = lax.axis_size("ta")
    same_core = [[t * 4 + z * 2 + c for t in range(n_ta) for z in range(2)] for c in range(2)]
    chips = [[0, 1], [2, 3]]
    vmem, smem, hbm = pltpu.VMEM, pltpu.SMEM, pltpu.HBM

    [packed] = call(
        pack_kernel,
        [vmem((256, WIDE), BF16)],
        [hbm] * 2,
        [pltpu.VMEM((32, 128), I32), pltpu.VMEM((SLOTS, WIDE), BF16)] + [pltpu.SemaphoreType.DMA] * 2,
        flops=10**7,
    )(plan, decoder_feature_rows)
    arrived = lax.all_to_all(
        packed.reshape(32, CAP, WIDE), ("ta", "ha"), 0, 0, axis_index_groups=same_core, tiled=True
    ).reshape(256, WIDE)
    weight, raw = (9, PAIR, WIDE), (9, 3 * OWN, CH)
    table, keep, wide, own, same_wide, same_own, select, second = call(
        prepare_kernel,
        [
            vmem((BLOCK, 512), BF16),
            vmem((EDGE + INNER, 2), BF16),
            vmem((2, CH), F32),
            vmem((4, PAIR), F32),
            vmem((CH, CH), BF16),
            vmem((PAIR, PAIR), BF16),
            vmem((PAIR, WIDE), BF16),
            hbm(weight, BF16),
        ],
        [smem] + [hbm] * 8,
        [vmem((32, 128), I32)] + [vmem((CH,), F32)] * 6 + [vmem(raw, BF16), pltpu.SemaphoreType.DMA((8,))],
        flops=2 * 10**9,
    )(
        latent_frame_count,
        plan,
        first_norm_gain,
        first_norm_bias,
        first_convolution_bias,
        second_norm_gain,
        second_norm_bias,
        second_convolution_bias,
        second_convolution_weight.reshape(raw),
    )
    both = lax.all_gather(arrived, "ha", axis=0, axis_index_groups=chips, tiled=True)
    [tail] = call(tail_kernel, [((EDGE, WIDE), BF16)], [vmem] * 2, flops=10**8)(table, both)
    earlier = lax.ppermute(tail, "ta", [(i, i + 1) for i in range(n_ta - 1)])
    act, rest, head, near = call(
        main_kernel,
        [
            vmem((FOLDED - CUT, 128), BF16),
            vmem((BLOCK, PAIR), BF16),
            vmem((3, 32, WIDE), BF16),
            vmem(weight, BF16),
        ],
        [vmem] * 9,
        [vmem((BLOCK, WIDE), BF16), vmem((3, BLOCK, WIDE), BF16)],
        flops=2 * 10**9,
    )(keep, table, both, wide, own, same_wide, same_own, select, first_convolution_weight.reshape(raw))
    [act] = call(
        halo_kernel, [((FOLDED, 128), BF16)], [vmem] * 9, [vmem((3, EDGE + 32, WIDE), BF16)], flops=10**9
    )(keep, earlier, head, wide, own, same_wide, same_own, near, act)
    acts = lax.all_gather(act, "ha", axis=0, tiled=False)
    [out] = call(
        last_kernel,
        [((4, 96, 128), BF16)],
        [vmem] * 5,
        [pltpu.VMEM((3, EDGE + INNER, WIDE), BF16)],
        flops=2 * 10**9,
    )(keep, acts, rest, own, second)
    parts = lax.all_to_all(out, "ha", 0, 0, tiled=True)
    [joined] = call(join_kernel, [((F_DEV, 4, 2, CH), BF16)], [vmem])(parts)
    return joined


def solution(mesh):
    in_specs = (
        P(("dp", "ta", "ha"), None),
        P("dp"),
        P("dp"),
        P(),
        P(),
        P(None, None, None, "ha", None),
        P(),
        P(),
        P(),
        P(None, None, None, "ha", None),
        P(),
    )
    out_specs = P(("dp", "ta"), "ha", None, None)
    return jax.shard_map(local, mesh=mesh, in_specs=in_specs, out_specs=out_specs, check_vma=False)
```

```python
import jax
import jax.numpy as jnp
from jax import lax
from jax.experimental import pallas as pl
from jax.experimental.pallas import tpu as pltpu
from jax.sharding import PartitionSpec as P

CH = 384
WIDE = 768
GROUP = 12
ROWS = 16
OWN = 96
PAIR = 192
F_DEV = 16
BLOCK = 256
SLOTS = 64
CAP = 8
PLACES = 2 * CAP
VIDEOS = 6
EDGE = 64
INNER = BLOCK - 2 * ROWS
HELD = EDGE + BLOCK
OUT = EDGE + INNER
FOLDED = OUT * 3 // 2
F32, BF16, I32 = jnp.float32, jnp.bfloat16, jnp.int32
VMEM_LIMIT = 24 * 2**20


def dot(a, b):
    return jnp.dot(a, b, preferred_element_type=F32)


def dot_nt(a, b):
    return lax.dot_general(a, b, (((1,), (1,)), ((), ())), preferred_element_type=F32)


def iota(shape, axis):
    return lax.broadcasted_iota(I32, shape, axis)


def twelfth(v):
    return (v * 43691) >> 19


def three(v):
    high = v.astype(BF16)
    rest = v - high.astype(F32)
    middle = rest.astype(BF16)
    low = (rest - middle.astype(F32)).astype(BF16)
    return high, middle, low


def place():
    return lax.axis_index("ta"), lax.axis_index("ha")


def pack_kernel(plan_hbm, rows_hbm, out_ref, plan_ref, rows_ref, plan_sem, rows_sem):
    plan_copy = pltpu.make_async_copy(plan_hbm, plan_ref, plan_sem)
    rows_copy = pltpu.make_async_copy(rows_hbm, rows_ref, rows_sem)
    plan_copy.start()
    rows_copy.start()
    ta, ha = place()
    own = ta * 4 + ha
    lower = (iota((128, 128), 0) < iota((128, 128), 1)).astype(BF16)
    spot = iota((32 * PLACES, 128), 0)
    late = (spot & 15) >= CAP
    spot = ((spot >> 5) - jnp.where(late, 1, 0)) * CAP + (spot & 7)
    plan_copy.wait()
    ids = plan_ref[pl.ds(own // 2, 1), :]
    ids = jnp.where(own % 2 == 1, pltpu.roll(ids, 64, 1), ids)
    block = ids >> 8
    last = (ids & 255) >= BLOCK - EDGE
    hit = jnp.where(iota((16, 128), 0) == block, 1.0, 0.0)
    edge = jnp.where(last, hit, 0.0)
    before = dot(jnp.concatenate([hit, edge], axis=0).astype(BF16), lower)
    rank = jnp.sum(hit * before[0:16], axis=0, keepdims=True).astype(I32)
    edge_rank = jnp.sum(edge * before[16:32], axis=0, keepdims=True).astype(I32)
    position = block * CAP + rank
    edge_position = jnp.where(last, block * CAP + edge_rank, -1000)
    hot = (spot == jnp.where(late, edge_position, position)).astype(BF16)
    rows_copy.wait()
    out_ref[...] = dot(hot[:, :SLOTS], rows_ref[...]).astype(BF16)


def same_group(lanes, wrap):
    first, second = iota((lanes, lanes), 0), iota((lanes, lanes), 1)
    if wrap < lanes:
        first = jnp.where(first >= wrap, first - wrap, first)
        second = jnp.where(second >= wrap, second - wrap, second)
    return (twelfth(first) == twelfth(second)).astype(BF16)


def side_by_side(weight_ref, out_ref):
    for tap in range(9):
        for c in range(2):
            out_ref[tap, :, c * CH : (c + 1) * CH] = weight_ref[tap, c * OWN : c * OWN + PAIR, :]


def prepare_kernel(
    count_ref, plan_hbm, gain_hbm, bias_hbm, b1_hbm, g2_hbm, n2_hbm, b2_hbm, w2_hbm,
    table_ref, keep_ref, wide_ref, own_ref, same_wide_ref, same_own_ref, select_ref, second_ref,
    plan_ref, gain_ref, bias_ref, b1_ref, g2_ref, n2_ref, b2_ref, w2_ref, sems,
):
    pairs = (
        (plan_hbm, plan_ref), (w2_hbm, w2_ref), (gain_hbm, gain_ref), (bias_hbm, bias_ref),
        (b1_hbm, b1_ref), (g2_hbm, g2_ref), (n2_hbm, n2_ref), (b2_hbm, b2_ref),
    )
    copies = [pltpu.make_async_copy(source, to, sems.at[k]) for k, (source, to) in enumerate(pairs)]
    for copy in copies:
        copy.start()
    ta, ha = place()
    frame = ta * F_DEV - 2 + (iota((OUT, 2), 0) >> 4)
    start = jnp.zeros((OUT, 2), I32)
    end = jnp.int32(0)
    for v in range(VIDEOS):
        count = count_ref[v]
        end = end + count
        start = start + jnp.where(frame >= end, count, 0)
    keep_ref[...] = jnp.where(frame - 2 + iota((OUT, 2), 1) >= start, 1.0, 0.0).astype(BF16)
    same_wide_ref[...] = same_group(CH, CH)
    same_own_ref[...] = same_group(PAIR, OWN)
    lane = iota((PAIR, WIDE), 0)
    source = ha * OWN + jnp.where(lane < OWN, CH + lane, lane - OWN)
    select_ref[...] = (iota((PAIR, WIDE), 1) == source).astype(BF16)
    copies[0].wait()
    plan = plan_ref[...]
    i, j = iota((128, 128), 0), iota((128, 128), 1)
    earlier = ((i < j) & ((i >> 6) == (j >> 6))).astype(BF16)
    place_in = plan & 255
    mine = (plan >> 8) == ta
    edge = ((plan >> 8) == ta - 1) & (place_in >= BLOCK - EDGE)
    ranked = []
    for match, value in ((mine, place_in + 1), (edge, place_in + 1 - (BLOCK - EDGE))):
        before = dot(match.astype(BF16), earlier)
        value = jnp.where(match, value, 0).astype(F32)
        ranked += [jnp.where(before == k, value, 0.0) for k in range(CAP)]
    half = ((iota((8, 128), 1) >> 6) == ha % 2).astype(BF16)
    held = dot_nt(half, jnp.concatenate(ranked, axis=0).astype(BF16))
    q, p = iota((512, 512), 0), iota((512, 512), 1)
    held = dot(held.astype(BF16), (q == (p & 15) * 32 + (p >> 4)).astype(BF16))[0:1]
    row, p = iota((HELD, 512), 0), iota((HELD, 512), 1)
    want = (row + 1 - jnp.where((p & 15) < CAP, EDGE, 0)).astype(F32)
    table_ref[...] = ((held == want) & (held > 0.0)).astype(BF16)
    for copy in copies[2:]:
        copy.wait()
    wide_ref[0:1] = gain_ref[...].reshape(1, CH)
    wide_ref[1:2] = bias_ref[...].reshape(1, CH)
    for k, ref in enumerate((b1_ref, g2_ref, n2_ref, b2_ref)):
        value = ref[...].reshape(1, CH)
        part = jnp.zeros((1, OWN), F32)
        for h in range(4):
            part = jnp.where(ha == h, value[:, h * OWN : (h + 1) * OWN], part)
        own_ref[k : k + 1] = jnp.concatenate([part, part], axis=1)
    copies[1].wait()
    side_by_side(w2_ref, second_ref)


def unpack_kernel(table_ref, packed_ref, out_ref):
    out_ref[...] = dot(table_ref[...], packed_ref[...]).astype(BF16)


def squares(values):
    wide = values.astype(F32)
    square = wide * wide
    high = square.astype(BF16)
    return high, (square - high.astype(F32)).astype(BF16)


def moments(total, total_squares):
    entries = ROWS * 2 * GROUP
    mean = total / entries
    return mean, lax.rsqrt(total_squares / entries - mean * mean + 1e-06)


def wide_stats(values, same):
    rows = values.shape[0]
    pick = ((iota((32, rows), 1) >> 4) == iota((32, rows), 0)).astype(BF16)
    high, low = squares(values)
    both = jnp.concatenate([dot(pick, values), dot(pick, high) + dot(pick, low)], axis=0)
    both = both[:, :CH] + both[:, CH:]
    total = dot(jnp.concatenate(three(both), axis=0), same)
    total = total[0:64] + total[64:128] + total[128:192]
    return moments(total[0:32], total[32:64])


def own_stats(values, same):
    rows = values.shape[0]
    total = dot(jnp.concatenate([values, *squares(values)], axis=0), same)
    by_frame = [
        jnp.sum(part.reshape(rows // ROWS, ROWS, PAIR), axis=1)
        for part in (total[:rows], total[rows : 2 * rows] + total[2 * rows :])
    ]
    return moments(*by_frame)


def silu(v):
    return v / (1.0 + jnp.exp(-v))


def store_taps(taps_ref, at, act):
    row = iota((ROWS, WIDE), 0)
    taps_ref[0, at : at + ROWS, :] = jnp.where(row == 0, 0.0, pltpu.roll(act, 1, 0)).astype(BF16)
    taps_ref[1, at : at + ROWS, :] = act.astype(BF16)
    taps_ref[2, at : at + ROWS, :] = jnp.where(row == ROWS - 1, 0.0, pltpu.roll(act, ROWS - 1, 0)).astype(BF16)


def norm_first(rows_ref, wide_ref, same, taps_ref):
    gain, bias = wide_ref[0:1], wide_ref[1:2]
    mean, inverse = wide_stats(rows_ref[...], same)
    for f in range(rows_ref.shape[0] // ROWS):
        value = rows_ref[f * ROWS : (f + 1) * ROWS, :].astype(F32)
        m, s = mean[f : f + 1], inverse[f : f + 1]
        halves = [
            silu((value[:, c * CH : (c + 1) * CH] - m) * s * gain + bias) for c in range(2)
        ]
        store_taps(taps_ref, f * ROWS, jnp.concatenate(halves, axis=1))


def convolve(taps_ref, product, rows, keep):
    totals = []
    for a in range(3):
        acc = None
        for b in range(3):
            part = product(taps_ref[b, a * ROWS : a * ROWS + rows, :], 3 * a + b)
            acc = part if acc is None else acc + part
        totals.append(acc)
    keep = keep.astype(F32)
    return totals[2] + totals[0] * keep[:, 0:1] + totals[1] * keep[:, 1:2]


def with_weights(weight_ref):
    return lambda values, tap: dot_nt(values, weight_ref[tap])


def fold(values):
    half = values.shape[0] // 2
    rest = values[:, 128:]
    return jnp.concatenate([values[:, :128], jnp.concatenate([rest[:half], rest[half:]], axis=1)], axis=0)


def norm_second(hidden, own_ref, same):
    gain, bias = own_ref[1:2], own_ref[2:3]
    mean, inverse = own_stats(hidden, same)
    acts = []
    for f in range(hidden.shape[0] // ROWS):
        value = hidden[f * ROWS : (f + 1) * ROWS].astype(F32)
        acts.append(silu((value - mean[f : f + 1]) * inverse[f : f + 1] * gain + bias))
    return fold(jnp.concatenate(acts, axis=0)).astype(BF16)


def main_kernel(
    keep_ref, parts_ref, wide_ref, own_ref, same_wide_ref, same_own_ref, select_ref, raw_ref,
    act_ref, rest_ref, rows_ref, taps_ref, weight_ref,
):
    rows_ref[...] = (parts_ref[0:HELD, :].astype(F32) + parts_ref[HELD:, :].astype(F32)).astype(BF16)
    side_by_side(raw_ref, weight_ref)
    norm_first(rows_ref, wide_ref, same_wide_ref[...], taps_ref)
    rest_ref[...] = dot_nt(rows_ref[EDGE:, :], select_ref[...]).astype(BF16)
    hidden = convolve(taps_ref, with_weights(weight_ref), OUT, keep_ref[...]) + own_ref[0:1]
    act_ref[...] = norm_second(hidden.astype(BF16), own_ref, same_own_ref[...])


def unfolded(ref, h, f):
    half = OUT // ROWS // 2
    low = OUT + (f % half) * ROWS
    lane = 64 * (f // half)
    return jnp.concatenate(
        [
            ref[h, f * ROWS : (f + 1) * ROWS, :].astype(F32),
            ref[h, low : low + ROWS, :].astype(F32)[:, lane : lane + 64],
        ],
        axis=1,
    )


def last_kernel(keep_ref, act_ref, rest_ref, own_ref, weight_ref, out_ref, taps_ref):
    for f in range(F_DEV + 2):
        parts = [unfolded(act_ref, h, f) for h in range(4)]
        whole = jnp.concatenate([p[:, OWN:] for p in parts] + [p[:, :OWN] for p in parts], axis=1)
        store_taps(taps_ref, f * ROWS, whole)
    total = convolve(taps_ref, with_weights(weight_ref), BLOCK, keep_ref[2 * ROWS :, :])
    total = (total + own_ref[3:4] + rest_ref[...].astype(F32)).astype(BF16)
    to, at = iota((BLOCK, BLOCK), 0), iota((BLOCK, BLOCK), 1)
    order = (((to >> 2) & 15) * ROWS + (to >> 6) * 4 + (to & 3) == at).astype(BF16)
    ordered = dot(order, total)
    for h in range(4):
        out_ref[h] = fold(ordered[h * 64 : (h + 1) * 64]).astype(BF16)


def join_kernel(parts_ref, out_ref):
    parts = []
    for h in range(4):
        part = parts_ref[h].astype(F32)
        rest = jnp.concatenate([part[64:96, 0:64], part[64:96, 64:128]], axis=0)
        parts.append(jnp.concatenate([part[0:64], rest], axis=1))
    zero = jnp.concatenate([p[:, OWN:] for p in parts], axis=1)
    one = jnp.concatenate([p[:, :OWN] for p in parts], axis=1)
    out_ref[...] = jnp.stack([zero, one], axis=1).astype(BF16).reshape(F_DEV, 4, 2, CH)


def call(kernel, outs, ins, scratch=(), flops=0):
    run = pl.pallas_call(
        kernel,
        out_shape=[jax.ShapeDtypeStruct(*o) if isinstance(o, tuple) else o for o in outs],
        in_specs=[pl.BlockSpec(memory_space=m) for m in ins],
        out_specs=[pl.BlockSpec(memory_space=pltpu.VMEM)] * len(outs),
        scratch_shapes=list(scratch),
        compiler_params=pltpu.CompilerParams(vmem_limit_bytes=VMEM_LIMIT),
        cost_estimate=pl.CostEstimate(flops=flops, bytes_accessed=2**20, transcendentals=0),
    )

    def pinned(*args):
        return run(
            *(pltpu.with_memory_space_constraint(a, pltpu.HBM) if m is pltpu.HBM else a for a, m in zip(args, ins))
        )

    return pinned


def local(
    decoder_feature_rows,
    slot_row_index,
    latent_frame_count,
    first_norm_gain,
    first_norm_bias,
    first_convolution_weight,
    first_convolution_bias,
    second_norm_gain,
    second_norm_bias,
    second_convolution_weight,
    second_convolution_bias,
):
    plan = slot_row_index.reshape(32, 128)
    n_ta = lax.axis_size("ta")
    same_core = [[t * 4 + z * 2 + c for t in range(n_ta) for z in range(2)] for c in range(2)]
    chips = [[0, 1], [2, 3]]
    vmem, smem, hbm = pltpu.VMEM, pltpu.SMEM, pltpu.HBM

    [packed] = call(
        pack_kernel,
        [vmem((32 * PLACES, WIDE), BF16)],
        [hbm] * 2,
        [pltpu.VMEM((32, 128), I32), pltpu.VMEM((SLOTS, WIDE), BF16)] + [pltpu.SemaphoreType.DMA] * 2,
        flops=10**7,
    )(plan, decoder_feature_rows)
    arrived = lax.all_to_all(
        packed.reshape(32, PLACES, WIDE), ("ta", "ha"), 0, 0, axis_index_groups=same_core, tiled=True
    ).reshape(32 * PLACES, WIDE)
    weight, raw = (9, PAIR, WIDE), (9, 3 * OWN, CH)
    table, keep, wide, own, same_wide, same_own, select, second = call(
        prepare_kernel,
        [
            vmem((HELD, 512), BF16),
            vmem((OUT, 2), BF16),
            vmem((2, CH), F32),
            vmem((4, PAIR), F32),
            vmem((CH, CH), BF16),
            vmem((PAIR, PAIR), BF16),
            vmem((PAIR, WIDE), BF16),
            hbm(weight, BF16),
        ],
        [smem] + [hbm] * 8,
        [vmem((32, 128), I32)] + [vmem((CH,), F32)] * 6 + [vmem(raw, BF16), pltpu.SemaphoreType.DMA((8,))],
        flops=2 * 10**9,
    )(
        latent_frame_count,
        plan,
        first_norm_gain,
        first_norm_bias,
        first_convolution_bias,
        second_norm_gain,
        second_norm_bias,
        second_convolution_bias,
        second_convolution_weight.reshape(raw),
    )
    [part] = call(unpack_kernel, [((HELD, WIDE), BF16)], [vmem] * 2, flops=10**8)(table, arrived)
    parts = lax.all_gather(part, "ha", axis=0, axis_index_groups=chips, tiled=True)
    act, rest = call(
        main_kernel,
        [((FOLDED, 128), BF16), vmem((BLOCK, PAIR), BF16)],
        [vmem] * 8,
        [vmem((HELD, WIDE), BF16), vmem((3, HELD, WIDE), BF16), vmem(weight, BF16)],
        flops=2 * 10**9,
    )(keep, parts, wide, own, same_wide, same_own, select, first_convolution_weight.reshape(raw))
    acts = lax.all_gather(act, "ha", axis=0, tiled=False)
    [out] = call(
        last_kernel,
        [((4, 96, 128), BF16)],
        [vmem] * 5,
        [vmem((3, OUT, WIDE), BF16)],
        flops=2 * 10**9,
    )(keep, acts, rest, own, second)
    parts = lax.all_to_all(out, "ha", 0, 0, tiled=True)
    [joined] = call(join_kernel, [((F_DEV, 4, 2, CH), BF16)], [vmem])(parts)
    return joined


def solution(mesh):
    in_specs = (
        P(("dp", "ta", "ha"), None),
        P("dp"),
        P("dp"),
        P(),
        P(),
        P(None, None, None, "ha", None),
        P(),
        P(),
        P(),
        P(None, None, None, "ha", None),
        P(),
    )
    out_specs = P(("dp", "ta"), "ha", None, None)
    return jax.shard_map(local, mesh=mesh, in_specs=in_specs, out_specs=out_specs, check_vma=False)
```

```python
import jax
import jax.numpy as jnp
from jax import lax
from jax.experimental import pallas as pl
from jax.experimental.pallas import tpu as pltpu
from jax.sharding import PartitionSpec as P

CH = 384
WIDE = 768
GROUP = 12
ROWS = 16
OWN = 96
PAIR = 192
F_DEV = 16
BLOCK = 256
SLOTS = 64
CAP = 8
VIDEOS = 6
EDGE = 64
INNER = BLOCK - 2 * ROWS
FOLDED = (EDGE + INNER) * 3 // 2
CUT = EDGE * 3 // 2
F32, BF16, I32 = jnp.float32, jnp.bfloat16, jnp.int32
VMEM_LIMIT = 24 * 2**20


def dot(a, b):
    return jnp.dot(a, b, preferred_element_type=F32)


def dot_nt(a, b):
    return lax.dot_general(a, b, (((1,), (1,)), ((), ())), preferred_element_type=F32)


def iota(shape, axis):
    return lax.broadcasted_iota(I32, shape, axis)


def twelfth(v):
    return (v * 43691) >> 19


def three(v):
    high = v.astype(BF16)
    rest = v - high.astype(F32)
    middle = rest.astype(BF16)
    low = (rest - middle.astype(F32)).astype(BF16)
    return high, middle, low


def place():
    return lax.axis_index("ta"), lax.axis_index("ha")


def pack_kernel(plan_hbm, rows_hbm, out_ref, plan_ref, rows_ref, plan_sem, rows_sem):
    plan_copy = pltpu.make_async_copy(plan_hbm, plan_ref, plan_sem)
    rows_copy = pltpu.make_async_copy(rows_hbm, rows_ref, rows_sem)
    plan_copy.start()
    rows_copy.start()
    ta, ha = place()
    own = ta * 4 + ha
    lower = (iota((128, 128), 0) < iota((128, 128), 1)).astype(BF16)
    spot = iota((256, 128), 0)
    spot = (spot >> 4) * CAP + (spot & 7)
    plan_copy.wait()
    ids = plan_ref[pl.ds(own // 2, 1), :]
    ids = jnp.where(own % 2 == 1, pltpu.roll(ids, 64, 1), ids)
    block = ids >> 8
    hit = iota((16, 128), 0) == block
    before = dot(hit.astype(BF16), lower)
    rank = jnp.sum(jnp.where(hit, before, 0.0), axis=0, keepdims=True)
    hot = (spot == block * CAP + rank.astype(I32)).astype(BF16)
    rows_copy.wait()
    out_ref[...] = dot(hot[:, :SLOTS], rows_ref[...]).astype(BF16)


def same_group(lanes, wrap):
    first, second = iota((lanes, lanes), 0), iota((lanes, lanes), 1)
    if wrap < lanes:
        first = jnp.where(first >= wrap, first - wrap, first)
        second = jnp.where(second >= wrap, second - wrap, second)
    return (twelfth(first) == twelfth(second)).astype(BF16)


def side_by_side(weight_ref, out_ref):
    for tap in range(9):
        for c in range(2):
            out_ref[tap, :, c * CH : (c + 1) * CH] = weight_ref[tap, c * OWN : c * OWN + PAIR, :]


def prepare_kernel(
    count_ref, plan_hbm, gain_hbm, bias_hbm, b1_hbm, g2_hbm, n2_hbm, b2_hbm, w2_hbm,
    table_ref, edge_ref, keep_ref, wide_ref, own_ref, same_wide_ref, same_own_ref, select_ref, second_ref,
    plan_ref, gain_ref, bias_ref, b1_ref, g2_ref, n2_ref, b2_ref, w2_ref, sems,
):
    pairs = (
        (plan_hbm, plan_ref), (w2_hbm, w2_ref), (gain_hbm, gain_ref), (bias_hbm, bias_ref),
        (b1_hbm, b1_ref), (g2_hbm, g2_ref), (n2_hbm, n2_ref), (b2_hbm, b2_ref),
    )
    copies = [pltpu.make_async_copy(source, to, sems.at[k]) for k, (source, to) in enumerate(pairs)]
    for copy in copies:
        copy.start()
    ta, ha = place()
    frame = ta * F_DEV - 2 + (iota((EDGE + INNER, 2), 0) >> 4)
    start = jnp.zeros((EDGE + INNER, 2), I32)
    end = jnp.int32(0)
    for v in range(VIDEOS):
        count = count_ref[v]
        end = end + count
        start = start + jnp.where(frame >= end, count, 0)
    keep_ref[...] = jnp.where(frame - 2 + iota((EDGE + INNER, 2), 1) >= start, 1.0, 0.0).astype(BF16)
    same_wide_ref[...] = same_group(CH, CH)
    same_own_ref[...] = same_group(PAIR, OWN)
    lane = iota((PAIR, WIDE), 0)
    source = ha * OWN + jnp.where(lane < OWN, CH + lane, lane - OWN)
    select_ref[...] = (iota((PAIR, WIDE), 1) == source).astype(BF16)
    copies[0].wait()
    plan = plan_ref[...]
    match = (plan >> 8) == ta
    i, j = iota((128, 128), 0), iota((128, 128), 1)
    before = dot(match.astype(BF16), ((i < j) & ((i >> 6) == (j >> 6))).astype(BF16))
    value = jnp.where(match, (plan & 255) + 1, 0).astype(F32)
    ranked = jnp.concatenate([jnp.where(before == k, value, 0.0) for k in range(CAP)], axis=0)
    half = ((iota((8, 128), 1) >> 6) == iota((8, 128), 0)).astype(BF16)
    held = dot_nt(half, ranked.astype(BF16))
    q, p = iota((256, 256), 0), iota((256, 256), 1)
    held = dot(held.astype(BF16), (q == (p & 7) * 32 + (p >> 3)).astype(BF16))
    want = (q + 1).astype(F32)
    table_ref[:, 0:256] = (held[0:1] == want).astype(BF16)
    table_ref[:, 256:512] = (held[1:2] == want).astype(BF16)
    here = jnp.where(ha % 2 == 0, held[0:1], held[1:2])
    edge_ref[...] = (here == want[BLOCK - EDGE :]).astype(BF16)
    for copy in copies[2:]:
        copy.wait()
    wide_ref[0:1] = gain_ref[...].reshape(1, CH)
    wide_ref[1:2] = bias_ref[...].reshape(1, CH)
    for k, ref in enumerate((b1_ref, g2_ref, n2_ref, b2_ref)):
        value = ref[...].reshape(1, CH)
        part = jnp.zeros((1, OWN), F32)
        for h in range(4):
            part = jnp.where(ha == h, value[:, h * OWN : (h + 1) * OWN], part)
        own_ref[k : k + 1] = jnp.concatenate([part, part], axis=1)
    copies[1].wait()
    side_by_side(w2_ref, second_ref)


def tail_kernel(table_ref, packed_ref, tail_ref):
    tail_ref[...] = dot(table_ref[...], packed_ref[...]).astype(BF16)


def squares(values):
    wide = values.astype(F32)
    square = wide * wide
    high = square.astype(BF16)
    return high, (square - high.astype(F32)).astype(BF16)


def moments(total, total_squares):
    entries = ROWS * 2 * GROUP
    mean = total / entries
    return mean, lax.rsqrt(jnp.maximum(total_squares / entries - mean * mean, 0.0) + 1e-06)


def wide_stats(values, same):
    rows = values.shape[0]
    pick = ((iota((16, rows), 1) >> 4) == iota((16, rows), 0)).astype(BF16)
    high, low = squares(values)
    both = jnp.concatenate([dot(pick, values), dot(pick, high) + dot(pick, low)], axis=0)
    both = both[:, :CH] + both[:, CH:]
    total = dot(jnp.concatenate(three(both), axis=0), same)
    total = total[0:32] + total[32:64] + total[64:96]
    return moments(total[0:16], total[16:32])


def own_stats(values, same):
    rows = values.shape[0]
    total = dot(jnp.concatenate([values, *squares(values)], axis=0), same)
    by_frame = [
        jnp.sum(part.reshape(rows // ROWS, ROWS, PAIR), axis=1)
        for part in (total[:rows], total[rows : 2 * rows] + total[2 * rows :])
    ]
    return moments(*by_frame)


def silu(v):
    return v / (1.0 + jnp.exp(-v))


def store_taps(taps_ref, at, act):
    row = iota((ROWS, WIDE), 0)
    taps_ref[0, at : at + ROWS, :] = jnp.where(row == 0, 0.0, pltpu.roll(act, 1, 0)).astype(BF16)
    taps_ref[1, at : at + ROWS, :] = act.astype(BF16)
    taps_ref[2, at : at + ROWS, :] = jnp.where(row == ROWS - 1, 0.0, pltpu.roll(act, ROWS - 1, 0)).astype(BF16)


def norm_first(rows_ref, wide_ref, same, taps_ref):
    gain, bias = wide_ref[0:1], wide_ref[1:2]
    mean, inverse = wide_stats(rows_ref[...], same)
    for f in range(rows_ref.shape[0] // ROWS):
        value = rows_ref[f * ROWS : (f + 1) * ROWS, :].astype(F32)
        m, s = mean[f : f + 1], inverse[f : f + 1]
        halves = [
            silu((value[:, c * CH : (c + 1) * CH] - m) * s * gain + bias) for c in range(2)
        ]
        store_taps(taps_ref, f * ROWS, jnp.concatenate(halves, axis=1))


def convolve(taps_ref, product, rows, keep):
    totals = []
    for a in range(3):
        acc = None
        for b in range(3):
            part = product(taps_ref[b, a * ROWS : a * ROWS + rows, :], 3 * a + b)
            acc = part if acc is None else acc + part
        totals.append(acc)
    keep = keep.astype(F32)
    return totals[2] + totals[0] * keep[:, 0:1] + totals[1] * keep[:, 1:2]


def with_weights(weight_ref):
    return lambda values, tap: dot_nt(values, weight_ref[tap])


def fold(values):
    half = values.shape[0] // 2
    rest = values[:, 128:]
    return jnp.concatenate([values[:, :128], jnp.concatenate([rest[:half], rest[half:]], axis=1)], axis=0)


def norm_second(hidden, own_ref, same):
    gain, bias = own_ref[1:2], own_ref[2:3]
    mean, inverse = own_stats(hidden, same)
    acts = []
    for f in range(hidden.shape[0] // ROWS):
        value = hidden[f * ROWS : (f + 1) * ROWS].astype(F32)
        acts.append(silu((value - mean[f : f + 1]) * inverse[f : f + 1] * gain + bias))
    return fold(jnp.concatenate(acts, axis=0)).astype(BF16)


def main_kernel(
    keep_ref, table_ref, packed_ref, wide_ref, own_ref, same_wide_ref, same_own_ref, select_ref, raw_ref,
    act_ref, rest_ref, head_ref, weight_ref, rows_ref, taps_ref,
):
    rows_ref[...] = dot(table_ref[...], packed_ref[...]).astype(BF16)
    side_by_side(raw_ref, weight_ref)
    norm_first(rows_ref, wide_ref, same_wide_ref[...], taps_ref)
    rest_ref[...] = dot_nt(rows_ref[...], select_ref[...]).astype(BF16)
    for b in range(3):
        head_ref[b] = taps_ref[b, 0:32, :]
    hidden = convolve(taps_ref, with_weights(weight_ref), INNER, keep_ref[EDGE:, :]) + own_ref[0:1]
    act_ref[...] = norm_second(hidden.astype(BF16), own_ref, same_own_ref[...])


def halo_kernel(
    keep_ref, earlier_ref, head_ref, wide_ref, own_ref, same_wide_ref, same_own_ref, weight_ref, main_ref,
    act_ref, taps_ref, rows_ref,
):
    rows_ref[...] = (earlier_ref[0:EDGE, :].astype(F32) + earlier_ref[EDGE:, :].astype(F32)).astype(BF16)
    norm_first(rows_ref, wide_ref, same_wide_ref[...], taps_ref)
    for b in range(3):
        taps_ref[b, EDGE : EDGE + 32, :] = head_ref[b]
    hidden = convolve(taps_ref, with_weights(weight_ref), EDGE, keep_ref[0:EDGE, :]) + own_ref[0:1]
    act_ref[0:CUT, :] = norm_second(hidden.astype(BF16), own_ref, same_own_ref[...])
    act_ref[CUT:FOLDED, :] = main_ref[...]


def unfolded(ref, h, base, frames, f):
    half = frames // 2
    low = base + frames * ROWS + (f % half) * ROWS
    lane = 64 * (f // half)
    return jnp.concatenate(
        [
            ref[h, base + f * ROWS : base + (f + 1) * ROWS, :].astype(F32),
            ref[h, low : low + ROWS, :].astype(F32)[:, lane : lane + 64],
        ],
        axis=1,
    )


def last_kernel(keep_ref, act_ref, rest_ref, own_ref, weight_ref, out_ref, taps_ref):
    for f in range(F_DEV + 2):
        parts = [
            unfolded(act_ref, h, 0, 4, f) if f < 4 else unfolded(act_ref, h, CUT, 14, f - 4) for h in range(4)
        ]
        whole = jnp.concatenate([p[:, OWN:] for p in parts] + [p[:, :OWN] for p in parts], axis=1)
        store_taps(taps_ref, f * ROWS, whole)
    total = convolve(taps_ref, with_weights(weight_ref), BLOCK, keep_ref[2 * ROWS :, :])
    total = (total + own_ref[3:4] + rest_ref[...].astype(F32)).astype(BF16)
    to, at = iota((BLOCK, BLOCK), 0), iota((BLOCK, BLOCK), 1)
    order = (((to >> 2) & 15) * ROWS + (to >> 6) * 4 + (to & 3) == at).astype(BF16)
    ordered = dot(order, total)
    for h in range(4):
        out_ref[h] = fold(ordered[h * 64 : (h + 1) * 64]).astype(BF16)


def join_kernel(parts_ref, out_ref):
    parts = []
    for h in range(4):
        part = parts_ref[h].astype(F32)
        rest = jnp.concatenate([part[64:96, 0:64], part[64:96, 64:128]], axis=0)
        parts.append(jnp.concatenate([part[0:64], rest], axis=1))
    zero = jnp.concatenate([p[:, OWN:] for p in parts], axis=1)
    one = jnp.concatenate([p[:, :OWN] for p in parts], axis=1)
    out_ref[...] = jnp.stack([zero, one], axis=1).astype(BF16).reshape(F_DEV, 4, 2, CH)


def call(kernel, outs, ins, scratch=(), flops=0):
    run = pl.pallas_call(
        kernel,
        out_shape=[jax.ShapeDtypeStruct(*o) if isinstance(o, tuple) else o for o in outs],
        in_specs=[pl.BlockSpec(memory_space=m) for m in ins],
        out_specs=[pl.BlockSpec(memory_space=pltpu.VMEM)] * len(outs),
        scratch_shapes=list(scratch),
        compiler_params=pltpu.CompilerParams(vmem_limit_bytes=VMEM_LIMIT),
        cost_estimate=pl.CostEstimate(flops=flops, bytes_accessed=2**20, transcendentals=0),
    )

    def pinned(*args):
        return run(
            *(pltpu.with_memory_space_constraint(a, pltpu.HBM) if m is pltpu.HBM else a for a, m in zip(args, ins))
        )

    return pinned


def local(
    decoder_feature_rows,
    slot_row_index,
    latent_frame_count,
    first_norm_gain,
    first_norm_bias,
    first_convolution_weight,
    first_convolution_bias,
    second_norm_gain,
    second_norm_bias,
    second_convolution_weight,
    second_convolution_bias,
):
    plan = slot_row_index.reshape(32, 128)
    n_ta = lax.axis_size("ta")
    same_core = [[t * 4 + z * 2 + c for t in range(n_ta) for z in range(2)] for c in range(2)]
    chips = [[0, 1], [2, 3]]
    vmem, smem, hbm = pltpu.VMEM, pltpu.SMEM, pltpu.HBM

    [packed] = call(
        pack_kernel,
        [vmem((256, WIDE), BF16)],
        [hbm] * 2,
        [pltpu.VMEM((32, 128), I32), pltpu.VMEM((SLOTS, WIDE), BF16)] + [pltpu.SemaphoreType.DMA] * 2,
        flops=10**7,
    )(plan, decoder_feature_rows)
    arrived = lax.all_to_all(
        packed.reshape(32, CAP, WIDE), ("ta", "ha"), 0, 0, axis_index_groups=same_core, tiled=True
    ).reshape(256, WIDE)
    weight, raw = (9, PAIR, WIDE), (9, 3 * OWN, CH)
    table, edge, keep, wide, own, same_wide, same_own, select, second = call(
        prepare_kernel,
        [
            vmem((BLOCK, 512), BF16),
            vmem((EDGE, BLOCK), BF16),
            vmem((EDGE + INNER, 2), BF16),
            vmem((2, CH), F32),
            vmem((4, PAIR), F32),
            vmem((CH, CH), BF16),
            vmem((PAIR, PAIR), BF16),
            vmem((PAIR, WIDE), BF16),
            hbm(weight, BF16),
        ],
        [smem] + [hbm] * 8,
        [vmem((32, 128), I32)] + [vmem((CH,), F32)] * 6 + [vmem(raw, BF16), pltpu.SemaphoreType.DMA((8,))],
        flops=2 * 10**9,
    )(
        latent_frame_count,
        plan,
        first_norm_gain,
        first_norm_bias,
        first_convolution_bias,
        second_norm_gain,
        second_norm_bias,
        second_convolution_bias,
        second_convolution_weight.reshape(raw),
    )
    [tail] = call(tail_kernel, [((EDGE, WIDE), BF16)], [vmem] * 2, flops=10**8)(edge, arrived)
    tail, arrived = lax.optimization_barrier((tail, arrived))
    earlier = lax.ppermute(tail, "ta", [(i, i + 1) for i in range(n_ta - 1)])
    both = lax.all_gather(arrived, "ha", axis=0, axis_index_groups=chips, tiled=True)
    act, rest, head, near = call(
        main_kernel,
        [
            vmem((FOLDED - CUT, 128), BF16),
            vmem((BLOCK, PAIR), BF16),
            vmem((3, 32, WIDE), BF16),
            vmem(weight, BF16),
        ],
        [vmem] * 9,
        [vmem((BLOCK, WIDE), BF16), vmem((3, BLOCK, WIDE), BF16)],
        flops=10**6,
    )(keep, table, both, wide, own, same_wide, same_own, select, first_convolution_weight.reshape(raw))
    earlier = lax.all_gather(earlier, "ha", axis=0, axis_index_groups=chips, tiled=True)
    [act] = call(
        halo_kernel, [((FOLDED, 128), BF16)], [vmem] * 9, [vmem((3, EDGE + 32, WIDE), BF16), vmem((EDGE, WIDE), BF16)], flops=10**9
    )(keep, earlier, head, wide, own, same_wide, same_own, near, act)
    acts = lax.all_gather(act, "ha", axis=0, tiled=False)
    [out] = call(
        last_kernel,
        [((4, 96, 128), BF16)],
        [vmem] * 5,
        [pltpu.VMEM((3, EDGE + INNER, WIDE), BF16)],
        flops=2 * 10**9,
    )(keep, acts, rest, own, second)
    parts = lax.all_to_all(out, "ha", 0, 0, tiled=True)
    [joined] = call(join_kernel, [((F_DEV, 4, 2, CH), BF16)], [vmem])(parts)
    return joined


def solution(mesh):
    in_specs = (
        P(("dp", "ta", "ha"), None),
        P("dp"),
        P("dp"),
        P(),
        P(),
        P(None, None, None, "ha", None),
        P(),
        P(),
        P(),
        P(None, None, None, "ha", None),
        P(),
    )
    out_specs = P(("dp", "ta"), "ha", None, None)
    return jax.shard_map(local, mesh=mesh, in_specs=in_specs, out_specs=out_specs, check_vma=False)
```

```python
import jax
import jax.numpy as jnp
from jax import lax
from jax.experimental import pallas as pl
from jax.experimental.pallas import tpu as pltpu
from jax.sharding import PartitionSpec as P

CH = 384
WIDE = 768
GROUP = 12
ROWS = 16
OWN = 96
PAIR = 192
F_DEV = 16
BLOCK = 256
SLOTS = 64
CAP = 8
VIDEOS = 6
EDGE = 64
INNER = BLOCK - 2 * ROWS
FOLDED = (EDGE + INNER) * 3 // 2
CUT = EDGE * 3 // 2
F32, BF16, I32 = jnp.float32, jnp.bfloat16, jnp.int32
VMEM_LIMIT = 24 * 2**20


def dot(a, b):
    return jnp.dot(a, b, preferred_element_type=F32)


def dot_nt(a, b):
    return lax.dot_general(a, b, (((1,), (1,)), ((), ())), preferred_element_type=F32)


def iota(shape, axis):
    return lax.broadcasted_iota(I32, shape, axis)


def twelfth(v):
    return (v * 43691) >> 19


def three(v):
    high = v.astype(BF16)
    rest = v - high.astype(F32)
    middle = rest.astype(BF16)
    low = (rest - middle.astype(F32)).astype(BF16)
    return high, middle, low


def place():
    return lax.axis_index("ta"), lax.axis_index("ha")


def pack_kernel(plan_hbm, rows_hbm, out_ref, plan_ref, rows_ref, plan_sem, rows_sem):
    plan_copy = pltpu.make_async_copy(plan_hbm, plan_ref, plan_sem)
    rows_copy = pltpu.make_async_copy(rows_hbm, rows_ref, rows_sem)
    plan_copy.start()
    rows_copy.start()
    ta, ha = place()
    own = ta * 4 + ha
    lower = (iota((128, 128), 0) < iota((128, 128), 1)).astype(BF16)
    spot = iota((256, 128), 0)
    spot = (spot >> 4) * CAP + (spot & 7)
    plan_copy.wait()
    ids = plan_ref[pl.ds(own // 2, 1), :]
    ids = jnp.where(own % 2 == 1, pltpu.roll(ids, 64, 1), ids)
    block = ids >> 8
    hit = iota((16, 128), 0) == block
    before = dot(hit.astype(BF16), lower)
    rank = jnp.sum(jnp.where(hit, before, 0.0), axis=0, keepdims=True)
    hot = (spot == block * CAP + rank.astype(I32)).astype(BF16)
    rows_copy.wait()
    out_ref[...] = dot(hot[:, :SLOTS], rows_ref[...]).astype(BF16)


def same_group(lanes, wrap):
    first, second = iota((lanes, lanes), 0), iota((lanes, lanes), 1)
    if wrap < lanes:
        first = jnp.where(first >= wrap, first - wrap, first)
        second = jnp.where(second >= wrap, second - wrap, second)
    return (twelfth(first) == twelfth(second)).astype(BF16)


def side_by_side(weight_ref, out_ref):
    for tap in range(9):
        for c in range(2):
            out_ref[tap, :, c * CH : (c + 1) * CH] = weight_ref[tap, c * OWN : c * OWN + PAIR, :]


def prepare_kernel(
    count_ref, plan_hbm, gain_hbm, bias_hbm, b1_hbm, g2_hbm, n2_hbm, b2_hbm, w2_hbm,
    table_ref, keep_ref, wide_ref, own_ref, same_wide_ref, same_own_ref, select_ref, second_ref,
    plan_ref, gain_ref, bias_ref, b1_ref, g2_ref, n2_ref, b2_ref, w2_ref, sems,
):
    pairs = (
        (plan_hbm, plan_ref), (w2_hbm, w2_ref), (gain_hbm, gain_ref), (bias_hbm, bias_ref),
        (b1_hbm, b1_ref), (g2_hbm, g2_ref), (n2_hbm, n2_ref), (b2_hbm, b2_ref),
    )
    copies = [pltpu.make_async_copy(source, to, sems.at[k]) for k, (source, to) in enumerate(pairs)]
    for copy in copies:
        copy.start()
    ta, ha = place()
    frame = ta * F_DEV - 2 + (iota((EDGE + INNER, 2), 0) >> 4)
    start = jnp.zeros((EDGE + INNER, 2), I32)
    end = jnp.int32(0)
    for v in range(VIDEOS):
        count = count_ref[v]
        end = end + count
        start = start + jnp.where(frame >= end, count, 0)
    keep_ref[...] = jnp.where(frame - 2 + iota((EDGE + INNER, 2), 1) >= start, 1.0, 0.0).astype(BF16)
    same_wide_ref[...] = same_group(CH, CH)
    same_own_ref[...] = same_group(PAIR, OWN)
    lane = iota((PAIR, WIDE), 0)
    source = ha * OWN + jnp.where(lane < OWN, CH + lane, lane - OWN)
    select_ref[...] = (iota((PAIR, WIDE), 1) == source).astype(BF16)
    copies[0].wait()
    plan = plan_ref[...]
    match = (plan >> 8) == ta
    i, j = iota((128, 128), 0), iota((128, 128), 1)
    before = dot(match.astype(BF16), ((i < j) & ((i >> 6) == (j >> 6))).astype(BF16))
    value = jnp.where(match, (plan & 255) + 1, 0).astype(F32)
    ranked = jnp.concatenate([jnp.where(before == k, value, 0.0) for k in range(CAP)], axis=0)
    half = ((iota((8, 128), 1) >> 6) == iota((8, 128), 0)).astype(BF16)
    held = dot_nt(half, ranked.astype(BF16))
    q, p = iota((256, 256), 0), iota((256, 256), 1)
    held = dot(held.astype(BF16), (q == (p & 7) * 32 + (p >> 3)).astype(BF16))
    want = (q + 1).astype(F32)
    table_ref[:, 0:256] = (held[0:1] == want).astype(BF16)
    table_ref[:, 256:512] = (held[1:2] == want).astype(BF16)
    for copy in copies[2:]:
        copy.wait()
    wide_ref[0:1] = gain_ref[...].reshape(1, CH)
    wide_ref[1:2] = bias_ref[...].reshape(1, CH)
    for k, ref in enumerate((b1_ref, g2_ref, n2_ref, b2_ref)):
        value = ref[...].reshape(1, CH)
        part = jnp.zeros((1, OWN), F32)
        for h in range(4):
            part = jnp.where(ha == h, value[:, h * OWN : (h + 1) * OWN], part)
        own_ref[k : k + 1] = jnp.concatenate([part, part], axis=1)
    copies[1].wait()
    side_by_side(w2_ref, second_ref)


def tail_kernel(table_ref, packed_ref, tail_ref):
    tail_ref[...] = dot(table_ref[BLOCK - EDGE :, :], packed_ref[...]).astype(BF16)


def squares(values):
    wide = values.astype(F32)
    square = wide * wide
    high = square.astype(BF16)
    return high, (square - high.astype(F32)).astype(BF16)


def moments(total, total_squares):
    entries = ROWS * 2 * GROUP
    mean = total / entries
    return mean, lax.rsqrt(jnp.maximum(total_squares / entries - mean * mean, 0.0) + 1e-06)


def wide_stats(values, same):
    rows = values.shape[0]
    pick = ((iota((16, rows), 1) >> 4) == iota((16, rows), 0)).astype(BF16)
    high, low = squares(values)
    both = jnp.concatenate([dot(pick, values), dot(pick, high) + dot(pick, low)], axis=0)
    both = both[:, :CH] + both[:, CH:]
    total = dot(jnp.concatenate(three(both), axis=0), same)
    total = total[0:32] + total[32:64] + total[64:96]
    return moments(total[0:16], total[16:32])


def own_stats(values, same):
    rows = values.shape[0]
    total = dot(jnp.concatenate([values, *squares(values)], axis=0), same)
    by_frame = [
        jnp.sum(part.reshape(rows // ROWS, ROWS, PAIR), axis=1)
        for part in (total[:rows], total[rows : 2 * rows] + total[2 * rows :])
    ]
    return moments(*by_frame)


def silu(v):
    return v / (1.0 + jnp.exp(-v))


def store_taps(taps_ref, at, act):
    row = iota((ROWS, WIDE), 0)
    taps_ref[0, at : at + ROWS, :] = jnp.where(row == 0, 0.0, pltpu.roll(act, 1, 0)).astype(BF16)
    taps_ref[1, at : at + ROWS, :] = act.astype(BF16)
    taps_ref[2, at : at + ROWS, :] = jnp.where(row == ROWS - 1, 0.0, pltpu.roll(act, ROWS - 1, 0)).astype(BF16)


def norm_first(rows_ref, wide_ref, same, taps_ref):
    gain, bias = wide_ref[0:1], wide_ref[1:2]
    mean, inverse = wide_stats(rows_ref[...], same)
    for f in range(rows_ref.shape[0] // ROWS):
        value = rows_ref[f * ROWS : (f + 1) * ROWS, :].astype(F32)
        m, s = mean[f : f + 1], inverse[f : f + 1]
        halves = [
            silu((value[:, c * CH : (c + 1) * CH] - m) * s * gain + bias) for c in range(2)
        ]
        store_taps(taps_ref, f * ROWS, jnp.concatenate(halves, axis=1))


def convolve(taps_ref, product, rows, keep):
    totals = []
    for a in range(3):
        acc = None
        for b in range(3):
            part = product(taps_ref[b, a * ROWS : a * ROWS + rows, :], 3 * a + b)
            acc = part if acc is None else acc + part
        totals.append(acc)
    keep = keep.astype(F32)
    return totals[2] + totals[0] * keep[:, 0:1] + totals[1] * keep[:, 1:2]


def with_weights(weight_ref):
    return lambda values, tap: dot_nt(values, weight_ref[tap])


def fold(values):
    half = values.shape[0] // 2
    rest = values[:, 128:]
    return jnp.concatenate([values[:, :128], jnp.concatenate([rest[:half], rest[half:]], axis=1)], axis=0)


def norm_second(hidden, own_ref, same):
    gain, bias = own_ref[1:2], own_ref[2:3]
    mean, inverse = own_stats(hidden, same)
    acts = []
    for f in range(hidden.shape[0] // ROWS):
        value = hidden[f * ROWS : (f + 1) * ROWS].astype(F32)
        acts.append(silu((value - mean[f : f + 1]) * inverse[f : f + 1] * gain + bias))
    return fold(jnp.concatenate(acts, axis=0)).astype(BF16)


def main_kernel(
    keep_ref, table_ref, packed_ref, wide_ref, own_ref, same_wide_ref, same_own_ref, select_ref, raw_ref,
    act_ref, rest_ref, head_ref, weight_ref, rows_ref, taps_ref,
):
    rows_ref[...] = dot(table_ref[...], packed_ref[...]).astype(BF16)
    side_by_side(raw_ref, weight_ref)
    norm_first(rows_ref, wide_ref, same_wide_ref[...], taps_ref)
    rest_ref[...] = dot_nt(rows_ref[...], select_ref[...]).astype(BF16)
    for b in range(3):
        head_ref[b] = taps_ref[b, 0:32, :]
    hidden = convolve(taps_ref, with_weights(weight_ref), INNER, keep_ref[EDGE:, :]) + own_ref[0:1]
    act_ref[...] = norm_second(hidden.astype(BF16), own_ref, same_own_ref[...])


def halo_kernel(
    keep_ref, earlier_ref, head_ref, wide_ref, own_ref, same_wide_ref, same_own_ref, weight_ref, main_ref,
    act_ref, taps_ref,
):
    norm_first(earlier_ref, wide_ref, same_wide_ref[...], taps_ref)
    for b in range(3):
        taps_ref[b, EDGE : EDGE + 32, :] = head_ref[b]
    hidden = convolve(taps_ref, with_weights(weight_ref), EDGE, keep_ref[0:EDGE, :]) + own_ref[0:1]
    act_ref[0:CUT, :] = norm_second(hidden.astype(BF16), own_ref, same_own_ref[...])
    act_ref[CUT:FOLDED, :] = main_ref[...]


def unfolded(ref, h, base, frames, f):
    half = frames // 2
    low = base + frames * ROWS + (f % half) * ROWS
    lane = 64 * (f // half)
    return jnp.concatenate(
        [
            ref[h, base + f * ROWS : base + (f + 1) * ROWS, :].astype(F32),
            ref[h, low : low + ROWS, :].astype(F32)[:, lane : lane + 64],
        ],
        axis=1,
    )


def last_kernel(keep_ref, act_ref, rest_ref, own_ref, weight_ref, out_ref, taps_ref):
    for f in range(F_DEV + 2):
        parts = [
            unfolded(act_ref, h, 0, 4, f) if f < 4 else unfolded(act_ref, h, CUT, 14, f - 4) for h in range(4)
        ]
        whole = jnp.concatenate([p[:, OWN:] for p in parts] + [p[:, :OWN] for p in parts], axis=1)
        store_taps(taps_ref, f * ROWS, whole)
    total = convolve(taps_ref, with_weights(weight_ref), BLOCK, keep_ref[2 * ROWS :, :])
    total = (total + own_ref[3:4] + rest_ref[...].astype(F32)).astype(BF16)
    to, at = iota((BLOCK, BLOCK), 0), iota((BLOCK, BLOCK), 1)
    order = (((to >> 2) & 15) * ROWS + (to >> 6) * 4 + (to & 3) == at).astype(BF16)
    ordered = dot(order, total)
    for h in range(4):
        out_ref[h] = fold(ordered[h * 64 : (h + 1) * 64]).astype(BF16)


def join_kernel(parts_ref, out_ref):
    parts = []
    for h in range(4):
        part = parts_ref[h].astype(F32)
        rest = jnp.concatenate([part[64:96, 0:64], part[64:96, 64:128]], axis=0)
        parts.append(jnp.concatenate([part[0:64], rest], axis=1))
    zero = jnp.concatenate([p[:, OWN:] for p in parts], axis=1)
    one = jnp.concatenate([p[:, :OWN] for p in parts], axis=1)
    out_ref[...] = jnp.stack([zero, one], axis=1).astype(BF16).reshape(F_DEV, 4, 2, CH)


def call(kernel, outs, ins, scratch=(), flops=0):
    run = pl.pallas_call(
        kernel,
        out_shape=[jax.ShapeDtypeStruct(*o) if isinstance(o, tuple) else o for o in outs],
        in_specs=[pl.BlockSpec(memory_space=m) for m in ins],
        out_specs=[pl.BlockSpec(memory_space=pltpu.VMEM)] * len(outs),
        scratch_shapes=list(scratch),
        compiler_params=pltpu.CompilerParams(vmem_limit_bytes=VMEM_LIMIT),
        cost_estimate=pl.CostEstimate(flops=flops, bytes_accessed=2**20, transcendentals=0),
    )

    def pinned(*args):
        return run(
            *(pltpu.with_memory_space_constraint(a, pltpu.HBM) if m is pltpu.HBM else a for a, m in zip(args, ins))
        )

    return pinned


def local(
    decoder_feature_rows,
    slot_row_index,
    latent_frame_count,
    first_norm_gain,
    first_norm_bias,
    first_convolution_weight,
    first_convolution_bias,
    second_norm_gain,
    second_norm_bias,
    second_convolution_weight,
    second_convolution_bias,
):
    plan = slot_row_index.reshape(32, 128)
    n_ta = lax.axis_size("ta")
    same_core = [[t * 4 + z * 2 + c for t in range(n_ta) for z in range(2)] for c in range(2)]
    chips = [[0, 1], [2, 3]]
    vmem, smem, hbm = pltpu.VMEM, pltpu.SMEM, pltpu.HBM

    [packed] = call(
        pack_kernel,
        [vmem((256, WIDE), BF16)],
        [hbm] * 2,
        [pltpu.VMEM((32, 128), I32), pltpu.VMEM((SLOTS, WIDE), BF16)] + [pltpu.SemaphoreType.DMA] * 2,
        flops=10**7,
    )(plan, decoder_feature_rows)
    arrived = lax.all_to_all(
        packed.reshape(32, CAP, WIDE), ("ta", "ha"), 0, 0, axis_index_groups=same_core, tiled=True
    ).reshape(256, WIDE)
    weight, raw = (9, PAIR, WIDE), (9, 3 * OWN, CH)
    table, keep, wide, own, same_wide, same_own, select, second = call(
        prepare_kernel,
        [
            vmem((BLOCK, 512), BF16),
            vmem((EDGE + INNER, 2), BF16),
            vmem((2, CH), F32),
            vmem((4, PAIR), F32),
            vmem((CH, CH), BF16),
            vmem((PAIR, PAIR), BF16),
            vmem((PAIR, WIDE), BF16),
            hbm(weight, BF16),
        ],
        [smem] + [hbm] * 8,
        [vmem((32, 128), I32)] + [vmem((CH,), F32)] * 6 + [vmem(raw, BF16), pltpu.SemaphoreType.DMA((8,))],
        flops=2 * 10**9,
    )(
        latent_frame_count,
        plan,
        first_norm_gain,
        first_norm_bias,
        first_convolution_bias,
        second_norm_gain,
        second_norm_bias,
        second_convolution_bias,
        second_convolution_weight.reshape(raw),
    )
    both = lax.all_gather(arrived, "ha", axis=0, axis_index_groups=chips, tiled=True)
    [tail] = call(tail_kernel, [((EDGE, WIDE), BF16)], [vmem] * 2, flops=10**8)(table, both)
    earlier = lax.ppermute(tail, "ta", [(i, i + 1) for i in range(n_ta - 1)])
    act, rest, head, near = call(
        main_kernel,
        [
            vmem((FOLDED - CUT, 128), BF16),
            vmem((BLOCK, PAIR), BF16),
            vmem((3, 32, WIDE), BF16),
            vmem(weight, BF16),
        ],
        [vmem] * 9,
        [vmem((BLOCK, WIDE), BF16), vmem((3, BLOCK, WIDE), BF16)],
        flops=2 * 10**9,
    )(keep, table, both, wide, own, same_wide, same_own, select, first_convolution_weight.reshape(raw))
    [act] = call(
        halo_kernel, [((FOLDED, 128), BF16)], [vmem] * 9, [vmem((3, EDGE + 32, WIDE), BF16)], flops=10**9
    )(keep, earlier, head, wide, own, same_wide, same_own, near, act)
    acts = lax.all_gather(act, "ha", axis=0, tiled=False)
    [out] = call(
        last_kernel,
        [((4, 96, 128), BF16)],
        [vmem] * 5,
        [pltpu.VMEM((3, EDGE + INNER, WIDE), BF16)],
        flops=2 * 10**9,
    )(keep, acts, rest, own, second)
    parts = lax.all_to_all(out, "ha", 0, 0, tiled=True)
    [joined] = call(join_kernel, [((F_DEV, 4, 2, CH), BF16)], [vmem])(parts)
    return joined


def solution(mesh):
    in_specs = (
        P(("dp", "ta", "ha"), None),
        P("dp"),
        P("dp"),
        P(),
        P(),
        P(None, None, None, "ha", None),
        P(),
        P(),
        P(),
        P(None, None, None, "ha", None),
        P(),
    )
    out_specs = P(("dp", "ta"), "ha", None, None)
    return jax.shard_map(local, mesh=mesh, in_specs=in_specs, out_specs=out_specs, check_vma=False)
```

```python
import jax
import jax.numpy as jnp
from jax import lax
from jax.experimental import pallas as pl
from jax.experimental.pallas import tpu as pltpu
from jax.sharding import PartitionSpec as P

CH = 384
WIDE = 768
GROUP = 12
ROWS = 16
OWN = 96
PAIR = 192
F_DEV = 16
BLOCK = 256
SLOTS = 64
CAP = 8
VIDEOS = 6
EDGE = 64
INNER = BLOCK - 2 * ROWS
FOLDED = (EDGE + INNER) * 3 // 2
CUT = EDGE * 3 // 2
F32, BF16, I32 = jnp.float32, jnp.bfloat16, jnp.int32
VMEM_LIMIT = 24 * 2**20


def dot(a, b):
    return jnp.dot(a, b, preferred_element_type=F32)


def dot_nt(a, b):
    return lax.dot_general(a, b, (((1,), (1,)), ((), ())), preferred_element_type=F32)


def iota(shape, axis):
    return lax.broadcasted_iota(I32, shape, axis)


def twelfth(v):
    return (v * 43691) >> 19


def three(v):
    high = v.astype(BF16)
    rest = v - high.astype(F32)
    middle = rest.astype(BF16)
    low = (rest - middle.astype(F32)).astype(BF16)
    return high, middle, low


def place():
    return lax.axis_index("ta"), lax.axis_index("ha")


def pack_kernel(plan_hbm, rows_hbm, out_ref, plan_ref, rows_ref, plan_sem, rows_sem):
    plan_copy = pltpu.make_async_copy(plan_hbm, plan_ref, plan_sem)
    rows_copy = pltpu.make_async_copy(rows_hbm, rows_ref, rows_sem)
    plan_copy.start()
    rows_copy.start()
    ta, ha = place()
    own = ta * 4 + ha
    lower = (iota((128, 128), 0) < iota((128, 128), 1)).astype(BF16)
    spot = iota((256, 128), 0)
    spot = (spot >> 4) * CAP + (spot & 7)
    plan_copy.wait()
    ids = plan_ref[pl.ds(own // 2, 1), :]
    ids = jnp.where(own % 2 == 1, pltpu.roll(ids, 64, 1), ids)
    block = ids >> 8
    hit = iota((16, 128), 0) == block
    before = dot(hit.astype(BF16), lower)
    rank = jnp.sum(jnp.where(hit, before, 0.0), axis=0, keepdims=True)
    hot = (spot == block * CAP + rank.astype(I32)).astype(BF16)
    rows_copy.wait()
    out_ref[...] = dot(hot[:, :SLOTS], rows_ref[...]).astype(BF16)


def same_group(lanes, wrap):
    first, second = iota((lanes, lanes), 0), iota((lanes, lanes), 1)
    if wrap < lanes:
        first = jnp.where(first >= wrap, first - wrap, first)
        second = jnp.where(second >= wrap, second - wrap, second)
    return (twelfth(first) == twelfth(second)).astype(BF16)


def side_by_side(weight_ref, out_ref):
    for tap in range(9):
        for c in range(2):
            out_ref[tap, :, c * CH : (c + 1) * CH] = weight_ref[tap, c * OWN : c * OWN + PAIR, :]


def prepare_kernel(
    count_ref, plan_hbm, gain_hbm, bias_hbm, b1_hbm, g2_hbm, n2_hbm, b2_hbm, w1_hbm, w2_hbm,
    table_ref, keep_ref, wide_ref, own_ref, same_wide_ref, same_own_ref, select_ref, first_ref, second_ref,
    plan_ref, gain_ref, bias_ref, b1_ref, g2_ref, n2_ref, b2_ref, w1_ref, w2_ref, sems,
):
    pairs = (
        (plan_hbm, plan_ref), (w1_hbm, w1_ref), (w2_hbm, w2_ref), (gain_hbm, gain_ref), (bias_hbm, bias_ref),
        (b1_hbm, b1_ref), (g2_hbm, g2_ref), (n2_hbm, n2_ref), (b2_hbm, b2_ref),
    )
    copies = [pltpu.make_async_copy(source, to, sems.at[k]) for k, (source, to) in enumerate(pairs)]
    for copy in copies:
        copy.start()
    ta, ha = place()
    frame = ta * F_DEV - 2 + (iota((EDGE + INNER, 2), 0) >> 4)
    start = jnp.zeros((EDGE + INNER, 2), I32)
    end = jnp.int32(0)
    for v in range(VIDEOS):
        count = count_ref[v]
        end = end + count
        start = start + jnp.where(frame >= end, count, 0)
    keep_ref[...] = jnp.where(frame - 2 + iota((EDGE + INNER, 2), 1) >= start, 1.0, 0.0).astype(BF16)
    same_wide_ref[...] = same_group(CH, CH)
    same_own_ref[...] = same_group(PAIR, OWN)
    lane = iota((PAIR, WIDE), 0)
    source = ha * OWN + jnp.where(lane < OWN, CH + lane, lane - OWN)
    select_ref[...] = (iota((PAIR, WIDE), 1) == source).astype(BF16)
    copies[0].wait()
    plan = plan_ref[...]
    match = (plan >> 8) == ta
    i, j = iota((128, 128), 0), iota((128, 128), 1)
    before = dot(match.astype(BF16), ((i < j) & ((i >> 6) == (j >> 6))).astype(BF16))
    value = jnp.where(match, (plan & 255) + 1, 0).astype(F32)
    ranked = jnp.concatenate([jnp.where(before == k, value, 0.0) for k in range(CAP)], axis=0)
    half = ((iota((8, 128), 1) >> 6) == iota((8, 128), 0)).astype(BF16)
    held = dot_nt(half, ranked.astype(BF16))
    q, p = iota((256, 256), 0), iota((256, 256), 1)
    held = dot(held.astype(BF16), (q == (p & 7) * 32 + (p >> 3)).astype(BF16))
    want = (q + 1).astype(F32)
    table_ref[:, 0:256] = (held[0:1] == want).astype(BF16)
    table_ref[:, 256:512] = (held[1:2] == want).astype(BF16)
    for copy in copies[3:]:
        copy.wait()
    wide_ref[0:1] = gain_ref[...].reshape(1, CH)
    wide_ref[1:2] = bias_ref[...].reshape(1, CH)
    for k, ref in enumerate((b1_ref, g2_ref, n2_ref, b2_ref)):
        value = ref[...].reshape(1, CH)
        part = jnp.zeros((1, OWN), F32)
        for h in range(4):
            part = jnp.where(ha == h, value[:, h * OWN : (h + 1) * OWN], part)
        own_ref[k : k + 1] = jnp.concatenate([part, part], axis=1)
    copies[1].wait()
    side_by_side(w1_ref, first_ref)
    copies[2].wait()
    side_by_side(w2_ref, second_ref)


def tail_kernel(table_ref, packed_ref, tail_ref):
    tail_ref[...] = dot(table_ref[BLOCK - EDGE :, :], packed_ref[...]).astype(BF16)


def squares(values):
    wide = values.astype(F32)
    square = wide * wide
    high = square.astype(BF16)
    return high, (square - high.astype(F32)).astype(BF16)


def moments(total, total_squares):
    entries = ROWS * 2 * GROUP
    mean = total / entries
    return mean, lax.rsqrt(jnp.maximum(total_squares / entries - mean * mean, 0.0) + 1e-06)


def wide_stats(values, same):
    rows = values.shape[0]
    pick = ((iota((16, rows), 1) >> 4) == iota((16, rows), 0)).astype(BF16)
    high, low = squares(values)
    both = jnp.concatenate([dot(pick, values), dot(pick, high) + dot(pick, low)], axis=0)
    both = both[:, :CH] + both[:, CH:]
    total = dot(jnp.concatenate(three(both), axis=0), same)
    total = total[0:32] + total[32:64] + total[64:96]
    return moments(total[0:16], total[16:32])


def own_stats(values, same):
    rows = values.shape[0]
    total = dot(jnp.concatenate([values, *squares(values)], axis=0), same)
    by_frame = [
        jnp.sum(part.reshape(rows // ROWS, ROWS, PAIR), axis=1)
        for part in (total[:rows], total[rows : 2 * rows] + total[2 * rows :])
    ]
    return moments(*by_frame)


def silu(v):
    return v / (1.0 + jnp.exp(-v))


def store_taps(taps_ref, at, act):
    row = iota((ROWS, WIDE), 0)
    taps_ref[0, at : at + ROWS, :] = jnp.where(row == 0, 0.0, pltpu.roll(act, 1, 0)).astype(BF16)
    taps_ref[1, at : at + ROWS, :] = act.astype(BF16)
    taps_ref[2, at : at + ROWS, :] = jnp.where(row == ROWS - 1, 0.0, pltpu.roll(act, ROWS - 1, 0)).astype(BF16)


def norm_first(rows_ref, wide_ref, same, taps_ref):
    gain, bias = wide_ref[0:1], wide_ref[1:2]
    mean, inverse = wide_stats(rows_ref[...], same)
    for f in range(rows_ref.shape[0] // ROWS):
        value = rows_ref[f * ROWS : (f + 1) * ROWS, :].astype(F32)
        m, s = mean[f : f + 1], inverse[f : f + 1]
        halves = [
            silu((value[:, c * CH : (c + 1) * CH] - m) * s * gain + bias) for c in range(2)
        ]
        store_taps(taps_ref, f * ROWS, jnp.concatenate(halves, axis=1))


def convolve(taps_ref, product, rows, keep):
    totals = []
    for a in range(3):
        acc = None
        for b in range(3):
            part = product(taps_ref[b, a * ROWS : a * ROWS + rows, :], 3 * a + b)
            acc = part if acc is None else acc + part
        totals.append(acc)
    keep = keep.astype(F32)
    return totals[2] + totals[0] * keep[:, 0:1] + totals[1] * keep[:, 1:2]


def with_weights(weight_ref):
    return lambda values, tap: dot_nt(values, weight_ref[tap])


def fold(values):
    half = values.shape[0] // 2
    rest = values[:, 128:]
    return jnp.concatenate([values[:, :128], jnp.concatenate([rest[:half], rest[half:]], axis=1)], axis=0)


def norm_second(hidden, own_ref, same):
    gain, bias = own_ref[1:2], own_ref[2:3]
    mean, inverse = own_stats(hidden, same)
    acts = []
    for f in range(hidden.shape[0] // ROWS):
        value = hidden[f * ROWS : (f + 1) * ROWS].astype(F32)
        acts.append(silu((value - mean[f : f + 1]) * inverse[f : f + 1] * gain + bias))
    return fold(jnp.concatenate(acts, axis=0)).astype(BF16)


def main_kernel(
    keep_ref, table_ref, packed_ref, wide_ref, own_ref, same_wide_ref, same_own_ref, select_hbm, weight_ref,
    act_ref, rest_ref, head_ref, rows_ref, taps_ref, select_ref, sem,
):
    copy = pltpu.make_async_copy(select_hbm, select_ref, sem)
    copy.start()
    rows_ref[...] = dot(table_ref[...], packed_ref[...]).astype(BF16)
    norm_first(rows_ref, wide_ref, same_wide_ref[...], taps_ref)
    copy.wait()
    rest_ref[...] = dot_nt(rows_ref[...], select_ref[...]).astype(BF16)
    for b in range(3):
        head_ref[b] = taps_ref[b, 0:32, :]
    hidden = convolve(taps_ref, with_weights(weight_ref), INNER, keep_ref[EDGE:, :]) + own_ref[0:1]
    act_ref[...] = norm_second(hidden.astype(BF16), own_ref, same_own_ref[...])


def halo_kernel(
    keep_ref, earlier_ref, head_ref, wide_ref, own_ref, same_wide_ref, same_own_ref, weight_ref, main_ref,
    act_ref, taps_ref,
):
    norm_first(earlier_ref, wide_ref, same_wide_ref[...], taps_ref)
    for b in range(3):
        taps_ref[b, EDGE : EDGE + 32, :] = head_ref[b]
    hidden = convolve(taps_ref, with_weights(weight_ref), EDGE, keep_ref[0:EDGE, :]) + own_ref[0:1]
    act_ref[0:CUT, :] = norm_second(hidden.astype(BF16), own_ref, same_own_ref[...])
    act_ref[CUT:FOLDED, :] = main_ref[...]


def unfolded(ref, h, base, frames, f):
    half = frames // 2
    low = base + frames * ROWS + (f % half) * ROWS
    lane = 64 * (f // half)
    return jnp.concatenate(
        [
            ref[h, base + f * ROWS : base + (f + 1) * ROWS, :].astype(F32),
            ref[h, low : low + ROWS, :].astype(F32)[:, lane : lane + 64],
        ],
        axis=1,
    )


def last_kernel(keep_ref, act_ref, rest_ref, own_ref, weight_ref, out_ref, taps_ref):
    for f in range(F_DEV + 2):
        parts = [
            unfolded(act_ref, h, 0, 4, f) if f < 4 else unfolded(act_ref, h, CUT, 14, f - 4) for h in range(4)
        ]
        whole = jnp.concatenate([p[:, OWN:] for p in parts] + [p[:, :OWN] for p in parts], axis=1)
        store_taps(taps_ref, f * ROWS, whole)
    total = convolve(taps_ref, with_weights(weight_ref), BLOCK, keep_ref[2 * ROWS :, :])
    total = (total + own_ref[3:4] + rest_ref[...].astype(F32)).astype(BF16)
    to, at = iota((BLOCK, BLOCK), 0), iota((BLOCK, BLOCK), 1)
    order = (((to >> 2) & 15) * ROWS + (to >> 6) * 4 + (to & 3) == at).astype(BF16)
    ordered = dot(order, total)
    for h in range(4):
        out_ref[h] = fold(ordered[h * 64 : (h + 1) * 64]).astype(BF16)


def join_kernel(parts_ref, out_ref):
    parts = []
    for h in range(4):
        part = parts_ref[h].astype(F32)
        rest = jnp.concatenate([part[64:96, 0:64], part[64:96, 64:128]], axis=0)
        parts.append(jnp.concatenate([part[0:64], rest], axis=1))
    zero = jnp.concatenate([p[:, OWN:] for p in parts], axis=1)
    one = jnp.concatenate([p[:, :OWN] for p in parts], axis=1)
    out_ref[...] = jnp.stack([zero, one], axis=1).astype(BF16).reshape(F_DEV, 4, 2, CH)


def call(kernel, outs, ins, scratch=(), flops=0):
    run = pl.pallas_call(
        kernel,
        out_shape=[jax.ShapeDtypeStruct(*o) if isinstance(o, tuple) else o for o in outs],
        in_specs=[pl.BlockSpec(memory_space=m) for m in ins],
        out_specs=[pl.BlockSpec(memory_space=pltpu.VMEM)] * len(outs),
        scratch_shapes=list(scratch),
        compiler_params=pltpu.CompilerParams(vmem_limit_bytes=VMEM_LIMIT),
        cost_estimate=pl.CostEstimate(flops=flops, bytes_accessed=2**20, transcendentals=0),
    )

    def pinned(*args):
        return run(
            *(pltpu.with_memory_space_constraint(a, pltpu.HBM) if m is pltpu.HBM else a for a, m in zip(args, ins))
        )

    return pinned


def local(
    decoder_feature_rows,
    slot_row_index,
    latent_frame_count,
    first_norm_gain,
    first_norm_bias,
    first_convolution_weight,
    first_convolution_bias,
    second_norm_gain,
    second_norm_bias,
    second_convolution_weight,
    second_convolution_bias,
):
    plan = slot_row_index.reshape(32, 128)
    n_ta = lax.axis_size("ta")
    same_core = [[t * 4 + z * 2 + c for t in range(n_ta) for z in range(2)] for c in range(2)]
    chips = [[0, 1], [2, 3]]
    vmem, smem, hbm = pltpu.VMEM, pltpu.SMEM, pltpu.HBM

    [packed] = call(
        pack_kernel,
        [vmem((256, WIDE), BF16)],
        [hbm] * 2,
        [pltpu.VMEM((32, 128), I32), pltpu.VMEM((SLOTS, WIDE), BF16)] + [pltpu.SemaphoreType.DMA] * 2,
        flops=10**7,
    )(plan, decoder_feature_rows)
    arrived = lax.all_to_all(
        packed.reshape(32, CAP, WIDE), ("ta", "ha"), 0, 0, axis_index_groups=same_core, tiled=True
    ).reshape(256, WIDE)
    weight, raw = (9, PAIR, WIDE), (9, 3 * OWN, CH)
    table, keep, wide, own, same_wide, same_own, select, first, second = call(
        prepare_kernel,
        [
            vmem((BLOCK, 512), BF16),
            vmem((EDGE + INNER, 2), BF16),
            vmem((2, CH), F32),
            vmem((4, PAIR), F32),
            vmem((CH, CH), BF16),
            vmem((PAIR, PAIR), BF16),
            hbm((PAIR, WIDE), BF16),
            vmem(weight, BF16),
            hbm(weight, BF16),
        ],
        [smem] + [hbm] * 9,
        [vmem((32, 128), I32)] + [vmem((CH,), F32)] * 6 + [vmem(raw, BF16)] * 2 + [pltpu.SemaphoreType.DMA((9,))],
        flops=2 * 10**9,
    )(
        latent_frame_count,
        plan,
        first_norm_gain,
        first_norm_bias,
        first_convolution_bias,
        second_norm_gain,
        second_norm_bias,
        second_convolution_bias,
        first_convolution_weight.reshape(raw),
        second_convolution_weight.reshape(raw),
    )
    both = lax.all_gather(arrived, "ha", axis=0, axis_index_groups=chips, tiled=True)
    [tail] = call(tail_kernel, [((EDGE, WIDE), BF16)], [vmem] * 2, flops=10**8)(table, both)
    earlier = lax.ppermute(tail, "ta", [(i, i + 1) for i in range(n_ta - 1)])
    act, rest, head = call(
        main_kernel,
        [
            vmem((FOLDED - CUT, 128), BF16),
            vmem((BLOCK, PAIR), BF16),
            vmem((3, 32, WIDE), BF16),
        ],
        [vmem] * 7 + [hbm, vmem],
        [vmem((BLOCK, WIDE), BF16), vmem((3, BLOCK, WIDE), BF16), vmem((PAIR, WIDE), BF16), pltpu.SemaphoreType.DMA],
        flops=2 * 10**9,
    )(keep, table, both, wide, own, same_wide, same_own, select, first)
    [act] = call(
        halo_kernel, [((FOLDED, 128), BF16)], [vmem] * 9, [vmem((3, EDGE + 32, WIDE), BF16)], flops=10**9
    )(keep, earlier, head, wide, own, same_wide, same_own, first, act)
    acts = lax.all_gather(act, "ha", axis=0, tiled=False)
    [out] = call(
        last_kernel,
        [((4, 96, 128), BF16)],
        [vmem] * 5,
        [pltpu.VMEM((3, EDGE + INNER, WIDE), BF16)],
        flops=2 * 10**9,
    )(keep, acts, rest, own, second)
    parts = lax.all_to_all(out, "ha", 0, 0, tiled=True)
    [joined] = call(join_kernel, [((F_DEV, 4, 2, CH), BF16)], [vmem])(parts)
    return joined


def solution(mesh):
    in_specs = (
        P(("dp", "ta", "ha"), None),
        P("dp"),
        P("dp"),
        P(),
        P(),
        P(None, None, None, "ha", None),
        P(),
        P(),
        P(),
        P(None, None, None, "ha", None),
        P(),
    )
    out_specs = P(("dp", "ta"), "ha", None, None)
    return jax.shard_map(local, mesh=mesh, in_specs=in_specs, out_specs=out_specs, check_vma=False)
```

```python
import jax
import jax.numpy as jnp
from jax import lax
from jax.experimental import pallas as pl
from jax.experimental.pallas import tpu as pltpu
from jax.sharding import PartitionSpec as P

CH = 384
WIDE = 768
GROUP = 12
ROWS = 16
OWN = 96
PAIR = 192
F_DEV = 16
BLOCK = 256
SLOTS = 64
CAP = 8
VIDEOS = 6
EDGE = 64
INNER = BLOCK - 2 * ROWS
FOLDED = (EDGE + INNER) * 3 // 2
CUT = EDGE * 3 // 2
F32, BF16, I32 = jnp.float32, jnp.bfloat16, jnp.int32
VMEM_LIMIT = 24 * 2**20


def dot(a, b):
    return jnp.dot(a, b, preferred_element_type=F32)


def dot_nt(a, b):
    return lax.dot_general(a, b, (((1,), (1,)), ((), ())), preferred_element_type=F32)


def iota(shape, axis):
    return lax.broadcasted_iota(I32, shape, axis)


def twelfth(v):
    return (v * 43691) >> 19


def three(v):
    high = v.astype(BF16)
    rest = v - high.astype(F32)
    middle = rest.astype(BF16)
    low = (rest - middle.astype(F32)).astype(BF16)
    return high, middle, low


def place():
    return lax.axis_index("ta"), lax.axis_index("ha")


def pack_kernel(plan_hbm, rows_hbm, out_ref, plan_ref, rows_ref, plan_sem, rows_sem):
    plan_copy = pltpu.make_async_copy(plan_hbm, plan_ref, plan_sem)
    rows_copy = pltpu.make_async_copy(rows_hbm, rows_ref, rows_sem)
    plan_copy.start()
    rows_copy.start()
    ta, ha = place()
    own = ta * 4 + ha
    lower = (iota((128, 128), 0) < iota((128, 128), 1)).astype(BF16)
    spot = iota((256, 128), 0)
    spot = (spot >> 4) * CAP + (spot & 7)
    plan_copy.wait()
    ids = plan_ref[pl.ds(own // 2, 1), :]
    ids = jnp.where(own % 2 == 1, pltpu.roll(ids, 64, 1), ids)
    block = ids >> 8
    hit = iota((16, 128), 0) == block
    before = dot(hit.astype(BF16), lower)
    rank = jnp.sum(jnp.where(hit, before, 0.0), axis=0, keepdims=True)
    hot = (spot == block * CAP + rank.astype(I32)).astype(BF16)
    rows_copy.wait()
    out_ref[...] = dot(hot[:, :SLOTS], rows_ref[...]).astype(BF16)


def same_group(lanes, wrap):
    first, second = iota((lanes, lanes), 0), iota((lanes, lanes), 1)
    if wrap < lanes:
        first = jnp.where(first >= wrap, first - wrap, first)
        second = jnp.where(second >= wrap, second - wrap, second)
    return (twelfth(first) == twelfth(second)).astype(BF16)


def side_by_side(weight_ref, out_ref):
    for tap in range(9):
        for c in range(2):
            out_ref[tap, :, c * CH : (c + 1) * CH] = weight_ref[tap, c * OWN : c * OWN + PAIR, :]


def prepare_kernel(
    count_ref, plan_hbm, gain_hbm, bias_hbm, b1_hbm, g2_hbm, n2_hbm, b2_hbm, w1_hbm, w2_hbm,
    table_ref, keep_ref, wide_ref, own_ref, same_wide_ref, same_own_ref, select_ref, first_ref, second_ref,
    plan_ref, gain_ref, bias_ref, b1_ref, g2_ref, n2_ref, b2_ref, w1_ref, w2_ref, sems,
):
    pairs = (
        (plan_hbm, plan_ref), (w1_hbm, w1_ref), (w2_hbm, w2_ref), (gain_hbm, gain_ref), (bias_hbm, bias_ref),
        (b1_hbm, b1_ref), (g2_hbm, g2_ref), (n2_hbm, n2_ref), (b2_hbm, b2_ref),
    )
    copies = [pltpu.make_async_copy(source, to, sems.at[k]) for k, (source, to) in enumerate(pairs)]
    for copy in copies:
        copy.start()
    ta, ha = place()
    frame = ta * F_DEV - 2 + (iota((EDGE + INNER, 2), 0) >> 4)
    start = jnp.zeros((EDGE + INNER, 2), I32)
    end = jnp.int32(0)
    for v in range(VIDEOS):
        count = count_ref[v]
        end = end + count
        start = start + jnp.where(frame >= end, count, 0)
    keep_ref[...] = jnp.where(frame - 2 + iota((EDGE + INNER, 2), 1) >= start, 1.0, 0.0).astype(BF16)
    same_wide_ref[...] = same_group(CH, CH)
    same_own_ref[...] = same_group(PAIR, OWN)
    lane = iota((PAIR, WIDE), 0)
    source = ha * OWN + jnp.where(lane < OWN, CH + lane, lane - OWN)
    select_ref[...] = (iota((PAIR, WIDE), 1) == source).astype(BF16)
    copies[0].wait()
    plan = plan_ref[...]
    match = (plan >> 8) == ta
    i, j = iota((128, 128), 0), iota((128, 128), 1)
    before = dot(match.astype(BF16), ((i < j) & ((i >> 6) == (j >> 6))).astype(BF16))
    value = jnp.where(match, (plan & 255) + 1, 0).astype(F32)
    ranked = jnp.concatenate([jnp.where(before == k, value, 0.0) for k in range(CAP)], axis=0)
    half = ((iota((8, 128), 1) >> 6) == iota((8, 128), 0)).astype(BF16)
    held = dot_nt(half, ranked.astype(BF16))
    q, p = iota((256, 256), 0), iota((256, 256), 1)
    held = dot(held.astype(BF16), (q == (p & 7) * 32 + (p >> 3)).astype(BF16))
    want = (q + 1).astype(F32)
    table_ref[:, 0:256] = (held[0:1] == want).astype(BF16)
    table_ref[:, 256:512] = (held[1:2] == want).astype(BF16)
    for copy in copies[3:]:
        copy.wait()
    wide_ref[0:1] = gain_ref[...].reshape(1, CH)
    wide_ref[1:2] = bias_ref[...].reshape(1, CH)
    for k, ref in enumerate((b1_ref, g2_ref, n2_ref, b2_ref)):
        value = ref[...].reshape(1, CH)
        part = jnp.zeros((1, OWN), F32)
        for h in range(4):
            part = jnp.where(ha == h, value[:, h * OWN : (h + 1) * OWN], part)
        own_ref[k : k + 1] = jnp.concatenate([part, part], axis=1)
    copies[1].wait()
    side_by_side(w1_ref, first_ref)
    copies[2].wait()
    side_by_side(w2_ref, second_ref)


def tail_kernel(table_ref, packed_ref, tail_ref):
    tail_ref[...] = dot(table_ref[BLOCK - EDGE :, :], packed_ref[...]).astype(BF16)


def squares(values):
    wide = values.astype(F32)
    square = wide * wide
    high = square.astype(BF16)
    return high, (square - high.astype(F32)).astype(BF16)


def moments(total, total_squares):
    entries = ROWS * 2 * GROUP
    mean = total / entries
    return mean, lax.rsqrt(jnp.maximum(total_squares / entries - mean * mean, 0.0) + 1e-06)


def wide_stats(values, same):
    rows = values.shape[0]
    pick = ((iota((16, rows), 1) >> 4) == iota((16, rows), 0)).astype(BF16)
    high, low = squares(values)
    both = jnp.concatenate([dot(pick, values), dot(pick, high) + dot(pick, low)], axis=0)
    both = both[:, :CH] + both[:, CH:]
    total = dot(jnp.concatenate(three(both), axis=0), same)
    total = total[0:32] + total[32:64] + total[64:96]
    return moments(total[0:16], total[16:32])


def own_stats(values, same):
    rows = values.shape[0]
    total = dot(jnp.concatenate([values, *squares(values)], axis=0), same)
    by_frame = [
        jnp.sum(part.reshape(rows // ROWS, ROWS, PAIR), axis=1)
        for part in (total[:rows], total[rows : 2 * rows] + total[2 * rows :])
    ]
    return moments(*by_frame)


def silu(v):
    return v / (1.0 + jnp.exp(-v))


def store_taps(taps_ref, at, act):
    row = iota((ROWS, WIDE), 0)
    taps_ref[0, at : at + ROWS, :] = jnp.where(row == 0, 0.0, pltpu.roll(act, 1, 0)).astype(BF16)
    taps_ref[1, at : at + ROWS, :] = act.astype(BF16)
    taps_ref[2, at : at + ROWS, :] = jnp.where(row == ROWS - 1, 0.0, pltpu.roll(act, ROWS - 1, 0)).astype(BF16)


def norm_first(rows_ref, wide_ref, same, taps_ref):
    gain, bias = wide_ref[0:1], wide_ref[1:2]
    mean, inverse = wide_stats(rows_ref[...], same)
    for f in range(rows_ref.shape[0] // ROWS):
        value = rows_ref[f * ROWS : (f + 1) * ROWS, :].astype(F32)
        m, s = mean[f : f + 1], inverse[f : f + 1]
        halves = [
            silu((value[:, c * CH : (c + 1) * CH] - m) * s * gain + bias) for c in range(2)
        ]
        store_taps(taps_ref, f * ROWS, jnp.concatenate(halves, axis=1))


def convolve(taps_ref, product, rows, keep):
    totals = []
    for a in range(3):
        acc = None
        for b in range(3):
            part = product(taps_ref[b, a * ROWS : a * ROWS + rows, :], 3 * a + b)
            acc = part if acc is None else acc + part
        totals.append(acc)
    keep = keep.astype(F32)
    return totals[2] + totals[0] * keep[:, 0:1] + totals[1] * keep[:, 1:2]


def with_weights(weight_ref):
    return lambda values, tap: dot_nt(values, weight_ref[tap])


def fold(values):
    half = values.shape[0] // 2
    rest = values[:, 128:]
    return jnp.concatenate([values[:, :128], jnp.concatenate([rest[:half], rest[half:]], axis=1)], axis=0)


def norm_second(hidden, own_ref, same):
    gain, bias = own_ref[1:2], own_ref[2:3]
    mean, inverse = own_stats(hidden, same)
    acts = []
    for f in range(hidden.shape[0] // ROWS):
        value = hidden[f * ROWS : (f + 1) * ROWS].astype(F32)
        acts.append(silu((value - mean[f : f + 1]) * inverse[f : f + 1] * gain + bias))
    return fold(jnp.concatenate(acts, axis=0)).astype(BF16)


def main_kernel(
    keep_ref, table_ref, packed_ref, wide_ref, own_ref, same_wide_ref, same_own_ref, select_hbm, weight_ref,
    act_ref, rest_ref, head_ref, rows_ref, taps_ref, select_ref, sem,
):
    copy = pltpu.make_async_copy(select_hbm, select_ref, sem)
    copy.start()
    rows_ref[...] = dot(table_ref[...], packed_ref[...]).astype(BF16)
    norm_first(rows_ref, wide_ref, same_wide_ref[...], taps_ref)
    for b in range(3):
        head_ref[b] = taps_ref[b, 0:32, :]
    hidden = convolve(taps_ref, with_weights(weight_ref), INNER, keep_ref[EDGE:, :]) + own_ref[0:1]
    act_ref[...] = norm_second(hidden.astype(BF16), own_ref, same_own_ref[...])
    copy.wait()
    rest_ref[...] = dot_nt(rows_ref[...], select_ref[...]).astype(BF16)


def halo_kernel(
    keep_ref, earlier_ref, head_ref, wide_ref, own_ref, same_wide_ref, same_own_ref, weight_ref, main_ref,
    act_ref, taps_ref,
):
    norm_first(earlier_ref, wide_ref, same_wide_ref[...], taps_ref)
    for b in range(3):
        taps_ref[b, EDGE : EDGE + 32, :] = head_ref[b]
    hidden = convolve(taps_ref, with_weights(weight_ref), EDGE, keep_ref[0:EDGE, :]) + own_ref[0:1]
    act_ref[0:CUT, :] = norm_second(hidden.astype(BF16), own_ref, same_own_ref[...])
    act_ref[CUT:FOLDED, :] = main_ref[...]


def unfolded(ref, h, base, frames, f):
    half = frames // 2
    low = base + frames * ROWS + (f % half) * ROWS
    lane = 64 * (f // half)
    return jnp.concatenate(
        [
            ref[h, base + f * ROWS : base + (f + 1) * ROWS, :].astype(F32),
            ref[h, low : low + ROWS, :].astype(F32)[:, lane : lane + 64],
        ],
        axis=1,
    )


def last_kernel(keep_ref, act_ref, rest_ref, own_ref, weight_ref, out_ref, taps_ref):
    for f in range(F_DEV + 2):
        parts = [
            unfolded(act_ref, h, 0, 4, f) if f < 4 else unfolded(act_ref, h, CUT, 14, f - 4) for h in range(4)
        ]
        whole = jnp.concatenate([p[:, OWN:] for p in parts] + [p[:, :OWN] for p in parts], axis=1)
        store_taps(taps_ref, f * ROWS, whole)
    total = convolve(taps_ref, with_weights(weight_ref), BLOCK, keep_ref[2 * ROWS :, :])
    total = (total + own_ref[3:4] + rest_ref[...].astype(F32)).astype(BF16)
    to, at = iota((BLOCK, BLOCK), 0), iota((BLOCK, BLOCK), 1)
    order = (((to >> 2) & 15) * ROWS + (to >> 6) * 4 + (to & 3) == at).astype(BF16)
    ordered = dot(order, total)
    for h in range(4):
        out_ref[h] = fold(ordered[h * 64 : (h + 1) * 64]).astype(BF16)


def join_kernel(parts_ref, out_ref):
    parts = []
    for h in range(4):
        part = parts_ref[h].astype(F32)
        rest = jnp.concatenate([part[64:96, 0:64], part[64:96, 64:128]], axis=0)
        parts.append(jnp.concatenate([part[0:64], rest], axis=1))
    zero = jnp.concatenate([p[:, OWN:] for p in parts], axis=1)
    one = jnp.concatenate([p[:, :OWN] for p in parts], axis=1)
    out_ref[...] = jnp.stack([zero, one], axis=1).astype(BF16).reshape(F_DEV, 4, 2, CH)


def call(kernel, outs, ins, scratch=(), flops=0):
    run = pl.pallas_call(
        kernel,
        out_shape=[jax.ShapeDtypeStruct(*o) if isinstance(o, tuple) else o for o in outs],
        in_specs=[pl.BlockSpec(memory_space=m) for m in ins],
        out_specs=[pl.BlockSpec(memory_space=pltpu.VMEM)] * len(outs),
        scratch_shapes=list(scratch),
        compiler_params=pltpu.CompilerParams(vmem_limit_bytes=VMEM_LIMIT),
        cost_estimate=pl.CostEstimate(flops=flops, bytes_accessed=2**20, transcendentals=0),
    )

    def pinned(*args):
        return run(
            *(pltpu.with_memory_space_constraint(a, pltpu.HBM) if m is pltpu.HBM else a for a, m in zip(args, ins))
        )

    return pinned


def local(
    decoder_feature_rows,
    slot_row_index,
    latent_frame_count,
    first_norm_gain,
    first_norm_bias,
    first_convolution_weight,
    first_convolution_bias,
    second_norm_gain,
    second_norm_bias,
    second_convolution_weight,
    second_convolution_bias,
):
    plan = slot_row_index.reshape(32, 128)
    n_ta = lax.axis_size("ta")
    same_core = [[t * 4 + z * 2 + c for t in range(n_ta) for z in range(2)] for c in range(2)]
    chips = [[0, 1], [2, 3]]
    vmem, smem, hbm = pltpu.VMEM, pltpu.SMEM, pltpu.HBM

    [packed] = call(
        pack_kernel,
        [vmem((256, WIDE), BF16)],
        [hbm] * 2,
        [pltpu.VMEM((32, 128), I32), pltpu.VMEM((SLOTS, WIDE), BF16)] + [pltpu.SemaphoreType.DMA] * 2,
        flops=10**7,
    )(plan, decoder_feature_rows)
    arrived = lax.all_to_all(
        packed.reshape(32, CAP, WIDE), ("ta", "ha"), 0, 0, axis_index_groups=same_core, tiled=True
    ).reshape(256, WIDE)
    weight, raw = (9, PAIR, WIDE), (9, 3 * OWN, CH)
    table, keep, wide, own, same_wide, same_own, select, first, second = call(
        prepare_kernel,
        [
            vmem((BLOCK, 512), BF16),
            vmem((EDGE + INNER, 2), BF16),
            vmem((2, CH), F32),
            vmem((4, PAIR), F32),
            vmem((CH, CH), BF16),
            vmem((PAIR, PAIR), BF16),
            hbm((PAIR, WIDE), BF16),
            vmem(weight, BF16),
            hbm(weight, BF16),
        ],
        [smem] + [hbm] * 9,
        [vmem((32, 128), I32)] + [vmem((CH,), F32)] * 6 + [vmem(raw, BF16)] * 2 + [pltpu.SemaphoreType.DMA((9,))],
        flops=2 * 10**9,
    )(
        latent_frame_count,
        plan,
        first_norm_gain,
        first_norm_bias,
        first_convolution_bias,
        second_norm_gain,
        second_norm_bias,
        second_convolution_bias,
        first_convolution_weight.reshape(raw),
        second_convolution_weight.reshape(raw),
    )
    both = lax.all_gather(arrived, "ha", axis=0, axis_index_groups=chips, tiled=True)
    [tail] = call(tail_kernel, [((EDGE, WIDE), BF16)], [vmem] * 2, flops=10**8)(table, both)
    earlier = lax.ppermute(tail, "ta", [(i, i + 1) for i in range(n_ta - 1)])
    act, rest, head = call(
        main_kernel,
        [
            vmem((FOLDED - CUT, 128), BF16),
            vmem((BLOCK, PAIR), BF16),
            vmem((3, 32, WIDE), BF16),
        ],
        [vmem] * 7 + [hbm, vmem],
        [vmem((BLOCK, WIDE), BF16), vmem((3, BLOCK, WIDE), BF16), vmem((PAIR, WIDE), BF16), pltpu.SemaphoreType.DMA],
        flops=2 * 10**9,
    )(keep, table, both, wide, own, same_wide, same_own, select, first)
    [act] = call(
        halo_kernel, [((FOLDED, 128), BF16)], [vmem] * 9, [vmem((3, EDGE + 32, WIDE), BF16)], flops=10**9
    )(keep, earlier, head, wide, own, same_wide, same_own, first, act)
    acts = lax.all_gather(act, "ha", axis=0, tiled=False)
    [out] = call(
        last_kernel,
        [((4, 96, 128), BF16)],
        [vmem] * 5,
        [pltpu.VMEM((3, EDGE + INNER, WIDE), BF16)],
        flops=2 * 10**9,
    )(keep, acts, rest, own, second)
    parts = lax.all_to_all(out, "ha", 0, 0, tiled=True)
    [joined] = call(join_kernel, [((F_DEV, 4, 2, CH), BF16)], [vmem])(parts)
    return joined


def solution(mesh):
    in_specs = (
        P(("dp", "ta", "ha"), None),
        P("dp"),
        P("dp"),
        P(),
        P(),
        P(None, None, None, "ha", None),
        P(),
        P(),
        P(),
        P(None, None, None, "ha", None),
        P(),
    )
    out_specs = P(("dp", "ta"), "ha", None, None)
    return jax.shard_map(local, mesh=mesh, in_specs=in_specs, out_specs=out_specs, check_vma=False)
```
